32 devices in a mesh: groups: 2 (over y), expert: 4 (over z), replica: 4 (over x, core).
Axes of the slice: x: 2, y: 2, z: 4, core: 2. Of those that a mesh axis runs over, the one named last changes fastest.
Arguments:
- tokens: bfloat16 [1024, 1024], P(('groups', 'expert')), parts along dimension 0, may hold values from -6 to 6
- out_grad: bfloat16 [1024, 1024], P(('groups', 'expert')), parts along dimension 0, may hold values from -6 to 6
- route_probs: float32 [1024, 6], P(('groups', 'expert')), parts along dimension 0, may hold values from 0.05 to 0.5
- routes: int32 [1024, 6], P(('groups', 'expert')), parts along dimension 0, may hold values from 0 to 63, all different within a row; in each aligned block of 128 rows (0 to 127, 128 to 255, ...) at most 16 rows name the same one
- placement: int32 [64], replicated, may hold values from 0 to 63, each once
- gate_weight: bfloat16 [64, 1024, 1408], P('expert', None, 'replica'), may hold values from -0.1875 to 0.1875
- up_weight: bfloat16 [64, 1024, 1408], P('expert', None, 'replica'), may hold values from -0.1875 to 0.1875
- down_weight: bfloat16 [64, 1408, 1024], P('expert', 'replica'), may hold values from -0.15625 to 0.15625
Outputs:
- layer_out: bfloat16 [1024, 1024], P(('groups', 'expert')), parts along dimension 0
- token_grad: bfloat16 [1024, 1024], P(('groups', 'expert')), parts along dimension 0
- prob_grad: float32 [1024, 6], P(('groups', 'expert')), parts along dimension 0
- gate_grad: bfloat16 [128, 1024, 1408], P(('groups', 'expert'), None, 'replica'), parts along dimension 0
- up_grad: bfloat16 [128, 1024, 1408], P(('groups', 'expert'), None, 'replica'), parts along dimension 0
- down_grad: bfloat16 [128, 1408, 1024], P(('groups', 'expert'), 'replica'), parts along dimension 0
The draws below stay inside these ranges and needn't reach their ends.
There are 2 independent parts, one for each index of `groups`. The reference program is written for one: setup_inputs(seed, part) draws one part's arguments, and reference() takes and returns one part's arrays. A program takes and returns all parts, laid end to end along the dimension named above; an argument that names none is the same for every part. Nothing has to cross between parts.
Inputs may be any that keep to these rules, and one draw needn't show every extreme that they name: `routes`: each row names 6 different experts. In the rows of one device (aligned blocks of 128 rows) no expert is named by more than 16 rows, and in some blocks one expert is named by exactly 16 rows. A permutation: expert e's weights are those of slot placement[e].
All inputs are finite; a program needn't handle non-finite values.
Results may differ from the reference program's by a relative error of at most 0.012.
Values may be sent and summed in bfloat16 or wider, within the bound.
A program may use at most 192 MiB of HBM per device.

```python
import math
import jax
import jax.numpy as jnp
import numpy as np
from jax import lax

D = 1024
H = 1408
EXPERTS = 64
TOP = 6
TOK_DEV = 128
MOST = 16
TOKENS = 512
N_EXPERT = 4
N_REPLICA = 4


def levels(own_key, extent, pieces, low, top_value):
    def one(position, shards_of):
        heights = jax.random.uniform(jax.random.fold_in(jax.random.fold_in(own_key, 6), position), (shards_of,), jnp.float32, low / len(pieces), top_value / len(pieces))
        return jnp.repeat(jnp.exp(heights), extent[position] // shards_of).reshape((-1,) + (1,) * (len(extent) - position - 1))

    gain = one(*pieces[0])
    for cut in pieces[1:]:
        gain = gain * one(*cut)
    return gain


def routed_block(stream_key, own, number, rows, number_of, top, reach, skew):
    sequence = jax.random.permutation(stream_key, number_of)
    crowded, ordinary = load_shares(number_of, rows * top, reach, skew, True), load_shares(number_of, rows * top, reach, skew, False)
    places = jnp.arange(number_of)

    def named(lengths, turn):
        used = int((lengths > 0).sum())
        fixed = max(1, used // 4)
        moved = fixed + (places - fixed + turn * (used - fixed)) % max(1, number_of - fixed)
        return jnp.zeros((number_of,), jnp.int32).at[sequence[jnp.where(places < fixed, places, moved)]].set(jnp.asarray(lengths, jnp.int32))

    lengths = jnp.where(number % 4 == 0, named(crowded, number // 4), named(ordinary, number - number // 4 - 1))
    mixed = jax.random.permutation(jax.random.fold_in(own, 3), number_of)
    source_of, receiver = mixed[0:number_of // 2 * 2:2], mixed[1:number_of // 2 * 2:2]
    slack = jnp.minimum(lengths[source_of] - 1, reach - lengths[receiver]) // 2
    slack = jnp.where((source_of == sequence[0]) | (receiver == sequence[0]) | (lengths[receiver] == 0), 0, jnp.maximum(slack, 0))
    moved = jax.random.randint(jax.random.fold_in(own, 4), (number_of // 2,), 0, 1 << 20) % (slack + 1)
    lengths = lengths.at[source_of].add(-moved).at[receiver].add(moved)
    members = jnp.searchsorted(jnp.cumsum(lengths), jnp.arange(rows * top), side="right").astype(jnp.int32)
    table = members.reshape(top, rows).T
    table = table[jax.random.permutation(jax.random.fold_in(own, 1), rows)]
    turn = jax.random.randint(jax.random.fold_in(own, 2), (rows, 1), 0, top)
    return jnp.take_along_axis(table, (jnp.arange(top)[None, :] + turn) % top, axis=1)


def load_shares(count, total, limit, slope, full):
    portions = [(1 << 20) // math.isqrt(grade ** slope) + 1 for grade in range(1, count + 1)]
    largest = limit if full else min(limit, max(-(-total // count), total * portions[0] // sum(portions)))
    least = 1 if total - largest >= count - 1 else 0
    given, rest = [largest] + [least] * (count - 1), total - largest - least * (count - 1)
    while rest > 0:
        candidates = [i for i in range(1, count) if given[i] < largest] or [i for i in range(1, count) if given[i] < limit]
        mass, remaining = sum([portions[i] for i in candidates]), rest
        for i in candidates:
            more = min(limit - given[i], max(1, remaining * portions[i] // mass), rest)
            given[i] = given[i] + more
            rest = rest - more
    return np.array(given)


def normal_values(stream_key, dims, width, bound, split=(), kind=jnp.bfloat16):
    drawn = jax.random.normal(stream_key, dims, jnp.float32) * width
    if len(split) > 0:
        drawn = levels(stream_key, dims, split, -0.22, 0.18) * drawn
    return jnp.clip(drawn, min=-bound, max=bound).astype(kind)


def setup_inputs(seed: int = 0, part: int = 0) -> dict:
    key_of = jax.random.split(jax.random.key(seed), 9)
    own_keys = jax.random.split(jax.random.fold_in(key_of[8], part), 9)
    tokens = normal_values(own_keys[0], (TOKENS, D), 1.0, 6.0, ((0, 4),))
    out_grad = normal_values(own_keys[1], (TOKENS, D), 1.0, 6.0, ((0, 4),))
    route_probs = jnp.clip(0.05 + 0.45 * jax.random.uniform(own_keys[2], (TOKENS, TOP), jnp.float32) ** levels(own_keys[2], (TOKENS, TOP), ((0, 4),), -0.2, 0.2), 0.05, 0.5)
    routes_keys = jax.random.split(jax.random.fold_in(own_keys[3], 1), TOKENS // TOK_DEV)
    routes_turns = jax.random.permutation(jax.random.fold_in(own_keys[3], 3), TOKENS // TOK_DEV)
    routes = jax.vmap(lambda own, number: routed_block(jax.random.fold_in(own_keys[3], 2), own, number, TOK_DEV, EXPERTS, TOP, MOST, 2))(routes_keys, routes_turns).reshape((TOKENS, TOP))
    placement = jax.random.permutation(key_of[4], EXPERTS).astype(jnp.int32)
    gate_weight = normal_values(key_of[5], (EXPERTS, D, H), D ** -0.5, 0.1875, ((0, 4), (2, 4)))
    up_weight = normal_values(key_of[6], (EXPERTS, D, H), D ** -0.5, 0.1875, ((0, 4), (2, 4)))
    down_weight = normal_values(key_of[7], (EXPERTS, H, D), H ** -0.5, 0.15625, ((0, 4), (1, 4)))
    return dict(tokens=tokens, out_grad=out_grad, route_probs=route_probs, routes=routes, placement=placement, gate_weight=gate_weight, up_weight=up_weight, down_weight=down_weight)


def quarter_sum(factor_pairs):
    left_first = factor_pairs[0][0]
    right_first = factor_pairs[0][1]
    quarter_size = left_first.shape[1] // N_REPLICA
    running = jnp.zeros((left_first.shape[0], right_first.shape[1]), jnp.float32)
    for quarter in range(N_REPLICA):
        lower = quarter * quarter_size
        upper_end = lower + quarter_size
        partial_value = jnp.zeros((left_first.shape[0], right_first.shape[1]), jnp.float32)
        for left_mat, right_mat in factor_pairs:
            partial_value = partial_value + jnp.dot(left_mat[:, lower:upper_end], right_mat[lower:upper_end], preferred_element_type=jnp.float32)
        rounded = lax.optimization_barrier(partial_value.astype(jnp.bfloat16))
        running = running + rounded.astype(jnp.float32)
    return running


def reference(tokens, out_grad, route_probs, routes, placement, gate_weight, up_weight, down_weight):
    top_k = routes.shape[1]
    experts_all = placement.shape[0]
    expert_ids = jnp.arange(experts_all, dtype=jnp.int32)
    route_slot = jnp.take(placement, routes.reshape(-1), axis=0).astype(jnp.int32)
    route_count = route_slot.shape[0]
    slot_counts = jnp.sum((route_slot[:, None] == expert_ids[None, :]).astype(jnp.int32), axis=0, dtype=jnp.int32)
    slot_starts = (jnp.cumsum(slot_counts, dtype=jnp.int32) - slot_counts).astype(jnp.int32)
    most_rows = N_EXPERT * MOST
    ordered = jnp.argsort(route_slot, stable=True).astype(jnp.int32)
    ordered = jnp.concatenate([ordered, jnp.zeros((most_rows,), jnp.int32)])
    probs_flat = route_probs.reshape(-1)
    row_ids = jnp.arange(most_rows, dtype=jnp.int32)

    def per_slot(totals, slot_id):
        layer_acc, token_acc, prob_acc = totals
        picked = lax.dynamic_slice_in_dim(ordered, slot_starts[slot_id].astype(jnp.int32), most_rows)
        live_rows = row_ids < slot_counts[slot_id]
        picked = jnp.where(live_rows, picked, 0).astype(jnp.int32)
        token_ids = (picked // top_k).astype(jnp.int32)
        input_rows = jnp.where(live_rows[:, None], tokens[token_ids], jnp.zeros((), tokens.dtype))
        weight_rows = jnp.where(live_rows, probs_flat[picked], jnp.zeros((), jnp.float32))
        grad_rows = out_grad[token_ids].astype(jnp.float32)
        route_grad = (weight_rows[:, None] * grad_rows).astype(jnp.bfloat16)
        gate_mat = gate_weight[slot_id]
        up_mat = up_weight[slot_id]
        down_mat = down_weight[slot_id]
        gate_pre = jnp.dot(input_rows, gate_mat, preferred_element_type=jnp.float32)
        up_pre = jnp.dot(input_rows, up_mat, preferred_element_type=jnp.float32)
        sigma_gate = jax.nn.sigmoid(gate_pre)
        swish_gate = gate_pre * sigma_gate
        hidden = (swish_gate * up_pre).astype(jnp.bfloat16)
        expert_out = quarter_sum(((hidden, down_mat),))
        hidden_grad = jnp.dot(route_grad, down_mat.T, preferred_element_type=jnp.float32)
        gate_back = (hidden_grad * up_pre * sigma_gate * (1.0 + gate_pre * (1.0 - sigma_gate))).astype(jnp.bfloat16)
        up_back = (hidden_grad * swish_gate).astype(jnp.bfloat16)
        input_grad = quarter_sum(((gate_back, gate_mat.T), (up_back, up_mat.T)))
        gate_grad = jnp.dot(input_rows.T, gate_back, preferred_element_type=jnp.float32).astype(jnp.bfloat16)
        up_grad = jnp.dot(input_rows.T, up_back, preferred_element_type=jnp.float32).astype(jnp.bfloat16)
        down_grad = jnp.dot(hidden.T, route_grad, preferred_element_type=jnp.float32).astype(jnp.bfloat16)
        live_col = live_rows[:, None]
        layer_acc = layer_acc.at[token_ids].add(jnp.where(live_col, weight_rows[:, None] * expert_out, jnp.zeros((), jnp.float32)))
        token_acc = token_acc.at[token_ids].add(jnp.where(live_col, input_grad, jnp.zeros((), jnp.float32)))
        prob_acc = prob_acc.at[picked].add(jnp.where(live_rows, jnp.sum(grad_rows * expert_out, axis=1), jnp.zeros((), jnp.float32)))
        return (layer_acc, token_acc, prob_acc), (gate_grad, up_grad, down_grad)

    start_carry = (jnp.zeros(tokens.shape, jnp.float32), jnp.zeros(tokens.shape, jnp.float32), jnp.zeros((route_count,), jnp.float32))
    finals, grads = lax.scan(per_slot, start_carry, expert_ids)
    layer_acc, token_acc, prob_acc = finals
    gate_grad, up_grad, down_grad = grads
    return (layer_acc.astype(jnp.bfloat16), token_acc.astype(jnp.bfloat16), prob_acc.reshape(routes.shape), gate_grad, up_grad, down_grad)
```

```python
import jax
import jax.numpy as jnp
from jax import lax
from jax.experimental import pallas as pl
from jax.experimental.pallas import tpu as pltpu
from jax.sharding import PartitionSpec as P

MOST = 16
MESH = pl.DeviceIdType.MESH


def expert_rows(input_rows, back_rows, gate_weight, up_weight, down_weight):
    gate_pre = jnp.einsum(
        "slcd,ldh->slch", input_rows, gate_weight, preferred_element_type=jnp.float32
    )
    up_pre = jnp.einsum("slcd,ldh->slch", input_rows, up_weight, preferred_element_type=jnp.float32)
    sigma_gate = jax.nn.sigmoid(gate_pre)
    swish_gate = gate_pre * sigma_gate
    hidden = (swish_gate * up_pre).astype(jnp.bfloat16)
    outputs = jnp.einsum("slch,lhd->slcd", hidden, down_weight, preferred_element_type=jnp.float32)
    hidden_grad = jnp.einsum(
        "slcd,lhd->slch", back_rows, down_weight, preferred_element_type=jnp.float32
    )
    gate_back = (hidden_grad * up_pre * sigma_gate * (1.0 + gate_pre * (1.0 - sigma_gate))).astype(
        jnp.bfloat16
    )
    up_back = (hidden_grad * swish_gate).astype(jnp.bfloat16)
    input_grad = jnp.einsum(
        "slch,ldh->slcd", gate_back, gate_weight, preferred_element_type=jnp.float32
    )
    input_grad = input_grad + jnp.einsum(
        "slch,ldh->slcd", up_back, up_weight, preferred_element_type=jnp.float32
    )
    return (outputs, input_grad, hidden, gate_back, up_back)


def shards(tokens, out_grad, route_probs, routes, placement, gate_weight, up_weight, down_weight):
    local_experts = gate_weight.shape[0]
    index_count = lax.axis_size("expert")
    experts_all = placement.shape[0]
    tok_rows, top_k = routes.shape
    model_width = tokens.shape[1]
    capacity = MOST
    expert_ids = jnp.arange(experts_all, dtype=jnp.int32)
    match_table = routes.reshape(-1)[:, None] == expert_ids[None, :]
    slot_ids = jnp.sum(jnp.where(match_table, placement[None, :], 0), axis=1, dtype=jnp.int32)
    slot_match = (slot_ids[:, None] == expert_ids[None, :]).astype(jnp.int32)
    rank_ids = jnp.sum(
        (jnp.cumsum(slot_match, axis=0, dtype=jnp.int32) - 1) * slot_match, axis=1, dtype=jnp.int32
    )
    position = slot_ids * capacity + rank_ids
    route_count = tok_rows * top_k
    buffer_rows = experts_all * capacity
    route_of = (
        jnp.full((buffer_rows,), route_count, jnp.int32)
        .at[position]
        .set(jnp.arange(route_count, dtype=jnp.int32))
    )
    filled = route_of < route_count
    safe_route = jnp.where(filled, route_of, 0)
    token_of = safe_route // top_k
    probs_flat = route_probs.reshape(-1)
    input_send = jnp.where(filled[:, None], tokens[token_of], jnp.zeros((), jnp.bfloat16))
    scaled = probs_flat[safe_route][:, None] * out_grad[token_of].astype(jnp.float32)
    back_send = jnp.where(filled[:, None], scaled, 0.0).astype(jnp.bfloat16)
    buffer_shape = (index_count, local_experts, capacity, model_width)
    input_send = input_send.reshape(buffer_shape)
    back_send = back_send.reshape(buffer_shape)
    input_piece = lax.all_to_all(input_send, "expert", split_axis=0, concat_axis=0, tiled=True)
    back_piece = lax.all_to_all(back_send, "expert", split_axis=0, concat_axis=0, tiled=True)
    results = expert_rows(input_piece, back_piece, gate_weight, up_weight, down_weight)
    input_rows, back_rows, outputs, input_grad, hidden, gate_back, up_back = (
        input_piece,
        back_piece,
    ) + results
    gate_grad = jnp.einsum(
        "slcd,slch->ldh", input_rows, gate_back, preferred_element_type=jnp.float32
    ).astype(jnp.bfloat16)
    up_grad = jnp.einsum(
        "slcd,slch->ldh", input_rows, up_back, preferred_element_type=jnp.float32
    ).astype(jnp.bfloat16)
    down_grad = jnp.einsum(
        "slch,slcd->lhd", hidden, back_rows, preferred_element_type=jnp.float32
    ).astype(jnp.bfloat16)
    out_back, grad_back = (
        lax.all_to_all(
            outputs.astype(jnp.bfloat16), "expert", split_axis=0, concat_axis=0, tiled=True
        ),
        lax.all_to_all(
            input_grad.astype(jnp.bfloat16), "expert", split_axis=0, concat_axis=0, tiled=True
        ),
    )
    kept_mask = rank_ids >= 0
    out_rows = out_back.reshape(-1, model_width)[position].astype(jnp.float32)
    grad_rows = grad_back.reshape(-1, model_width)[position].astype(jnp.float32)
    kept_rows = kept_mask.reshape(tok_rows, top_k)
    route_weight = jnp.where(kept_mask, probs_flat, 0.0).reshape(tok_rows, top_k)
    out_rows = out_rows.reshape(tok_rows, top_k, model_width)
    grad_rows = grad_rows.reshape(tok_rows, top_k, model_width)
    layer_part = jnp.sum(route_weight[:, :, None] * out_rows, axis=1)
    token_part = jnp.sum(jnp.where(kept_rows[:, :, None], grad_rows, 0.0), axis=1)
    prob_part = jnp.where(
        kept_rows, jnp.sum(out_grad.astype(jnp.float32)[:, None, :] * out_rows, axis=2), 0.0
    )
    layer_sum, token_sum, prob_sum = (
        lax.psum(layer_part.astype(jnp.bfloat16), "replica").astype(jnp.float32),
        lax.psum(token_part.astype(jnp.bfloat16), "replica").astype(jnp.float32),
        lax.psum(prob_part.astype(jnp.bfloat16), "replica").astype(jnp.float32),
    )
    return (
        layer_sum.astype(jnp.bfloat16),
        token_sum.astype(jnp.bfloat16),
        prob_sum,
        gate_grad,
        up_grad,
        down_grad,
    )


def place(expert=None, replica=None):
    own = [lax.axis_index("groups"), lax.axis_index("expert"), lax.axis_index("replica")]
    if expert is not None:
        own[1] = expert
    if replica is not None:
        own[2] = replica
    return tuple(own)


def greet(devices):
    barrier = pltpu.get_barrier_semaphore()
    for device in devices:
        pl.semaphore_signal(barrier, inc=1, device_id=device, device_id_type=MESH)
    pl.semaphore_wait(barrier, len(devices))


def positions():
    e, r = lax.axis_index("expert"), lax.axis_index("replica")
    core = r + 1 - 2 * lax.rem(r, 2)
    across = lax.rem(r + 2, 4)
    diagonal = lax.rem(core + 2, 4)
    return e, r, core, across, diagonal


def remote(src, dst, send, recv, device):
    copy = pltpu.make_async_remote_copy(
        src_ref=src, dst_ref=dst, send_sem=send, recv_sem=recv, device_id=device, device_id_type=MESH
    )
    copy.start()
    return copy


def gather_kernel(x_ref, g_ref, m_ref, rows_ref, meta_ref, send, recv):
    e, r, core, across, _ = positions()
    quarter = x_ref.shape[0] // 4
    greet(
        [place(expert=lax.rem(e + j, 4)) for j in (1, 2, 3)]
        + [place(replica=core), place(replica=across)]
    )
    rows_ref[e, 0] = x_ref[...]
    rows_ref[e, 1] = g_ref[...]
    meta_ref[e] = m_ref[...]
    mine = pl.ds(pl.multiple_of(r * quarter, quarter), quarter)
    other = pl.ds(pl.multiple_of(across * quarter, quarter), quarter)
    first, metas = {}, {}
    for j in (2, 1, 3):
        peer = place(expert=lax.rem(e + j, 4))
        own = rows_ref.at[e, :, mine]
        metas[j] = remote(meta_ref.at[e], meta_ref.at[e], send.at[0, j], recv.at[0, j], peer)
        first[j] = remote(own, own, send.at[1, j], recv.at[1, j], peer)
    passed, spread, last = {}, {}, {}
    for j in (1, 3, 2):
        block = lax.rem(e + 4 - j, 4)
        first[j].wait_recv()
        part = rows_ref.at[block, :, mine]
        passed[j] = remote(part, part, send.at[2, j], recv.at[2, j], place(replica=across))
        spread[j] = remote(part, part, send.at[3, j], recv.at[3, j], place(replica=core))
    for j in (1, 3, 2):
        block = lax.rem(e + 4 - j, 4)
        passed[j].wait_recv()
        part = rows_ref.at[block, :, other]
        last[j] = remote(part, part, send.at[4, j], recv.at[4, j], place(replica=core))
    for j in (1, 3, 2):
        metas[j].wait()
        first[j].wait_send()
        passed[j].wait_send()
        spread[j].wait()
        last[j].wait()


def gather_all(tokens, out_grad, meta):
    block, width = tokens.shape
    return pl.pallas_call(
        gather_kernel,
        out_shape=(
            jax.ShapeDtypeStruct((4, 2, block, width), jnp.bfloat16),
            jax.ShapeDtypeStruct((4,) + meta.shape, jnp.float32),
        ),
        in_specs=[pl.BlockSpec(memory_space=pltpu.VMEM)] * 3,
        out_specs=[pl.BlockSpec(memory_space=pltpu.VMEM)] * 2,
        scratch_shapes=[pltpu.SemaphoreType.DMA((5, 4)), pltpu.SemaphoreType.DMA((5, 4))],
        compiler_params=pltpu.CompilerParams(
            collective_id=0, has_side_effects=True, vmem_limit_bytes=24 * 2**20
        ),
    )(tokens, out_grad, meta)


def dot(left, right, left_dim, right_dim):
    return lax.dot_general(
        left, right, (((left_dim,), (right_dim,)), ((), ())), preferred_element_type=jnp.float32
    )


def slot_kernel(
    rows_ref, meta_ref, gate_ref, up_ref, down_ref,
    gate_out, up_out, down_out, part_ref, prob_ref,
    x_rows, g_rows, out_rows, grad_rows, pick_ref, weight_ref, inner_ref,
):
    s = pl.program_id(0)
    slots = pl.num_programs(0)
    block = rows_ref.shape[2]
    width = rows_ref.shape[3]
    top = 6
    held = slots * MOST
    base = lax.axis_index("expert") * slots

    def slot_names():
        names = lax.broadcasted_iota(jnp.int32, (slots, block), 0) + base
        return names.astype(jnp.float32)

    @pl.when(s == 0)
    def _():
        names = slot_names()
        before = lax.broadcasted_iota(jnp.int32, (block, block), 0)
        after = lax.broadcasted_iota(jnp.int32, (block, block), 1)
        earlier = (before < after).astype(jnp.float32).astype(jnp.bfloat16)
        ranks = lax.broadcasted_iota(jnp.int32, (slots, MOST, block), 1).astype(jnp.float32)
        for b in range(4):
            named = jnp.zeros((slots, block), jnp.float32)
            probs = jnp.zeros((slots, block), jnp.float32)
            for k in range(top):
                same = meta_ref[b, k : k + 1, :] == names
                named = named + jnp.where(same, 1.0, 0.0)
                probs = probs + jnp.where(same, meta_ref[b, 8 + k : 9 + k, :], 0.0)
            rank = dot(named.astype(jnp.bfloat16), earlier, 1, 0)
            rank = jnp.where(named > 0.0, rank, -1.0)
            pick = jnp.where(rank[:, None, :] == ranks, 1.0, 0.0)
            weight_ref[:, b] = jnp.sum(pick * probs[:, None, :], axis=2, keepdims=True)
            chosen = pick.reshape(held, block).astype(jnp.bfloat16)
            pick_ref[b] = chosen
            x_rows[:, b] = (
                dot(chosen, rows_ref[b, 0], 1, 0).astype(jnp.bfloat16).reshape(slots, MOST, width)
            )
            g_rows[:, b] = (
                dot(chosen, rows_ref[b, 1], 1, 0).astype(jnp.bfloat16).reshape(slots, MOST, width)
            )

    x = x_rows[s].reshape(4 * MOST, width)
    g = g_rows[s].reshape(4 * MOST, width)
    weight = weight_ref[s].reshape(4 * MOST, 1)
    gate_w, up_w, down_w = gate_ref[0], up_ref[0], down_ref[0]
    gate_pre = dot(x, gate_w, 1, 0)
    up_pre = dot(x, up_w, 1, 0)
    plain_grad = dot(g, down_w, 1, 1)
    sigma = jax.nn.sigmoid(gate_pre)
    swish = gate_pre * sigma
    hidden = (swish * up_pre).astype(jnp.bfloat16).astype(jnp.float32)
    inner = jnp.sum(hidden * plain_grad, axis=1, keepdims=True)
    inner_ref[s] = inner.reshape(4, MOST, 1)
    hidden_grad = plain_grad * weight
    gate_back = (hidden_grad * up_pre * sigma * (1.0 + gate_pre * (1.0 - sigma))).astype(
        jnp.bfloat16
    )
    up_back = (hidden_grad * swish).astype(jnp.bfloat16)
    scaled = (hidden * weight).astype(jnp.bfloat16)
    output = dot(scaled, down_w, 1, 0).astype(jnp.bfloat16).reshape(4, MOST, width)
    input_grad = dot(gate_back, gate_w, 1, 1) + dot(up_back, up_w, 1, 1)
    input_grad = input_grad.astype(jnp.bfloat16).reshape(4, MOST, width)
    for b in range(4):
        out_rows[b, s] = output[b]
        grad_rows[b, s] = input_grad[b]
    gate_out[0] = dot(x, gate_back, 0, 0).astype(jnp.bfloat16)
    up_out[0] = dot(x, up_back, 0, 0).astype(jnp.bfloat16)
    down_out[0] = dot(scaled, g, 0, 0).astype(jnp.bfloat16)

    @pl.when(s == slots - 1)
    def _():
        names = slot_names()
        quarter = block // 4
        for b in range(4):
            chosen = pick_ref[b]
            for a, held_rows in ((0, out_rows), (1, grad_rows)):
                total = dot(chosen, held_rows[b].reshape(held, width), 0, 0).astype(jnp.bfloat16)
                for q in range(4):
                    part_ref[q, b, a] = total[q * quarter : (q + 1) * quarter]
            pick = chosen.astype(jnp.float32).reshape(slots, MOST, block)
            inner_of = jnp.sum(pick * inner_ref[:, b], axis=1)
            for k in range(top):
                same = meta_ref[b, k : k + 1, :] == names
                prob_ref[b, k : k + 1, :] = jnp.sum(
                    jnp.where(same, inner_of, 0.0), axis=0, keepdims=True
                )
            prob_ref[b, top:8, :] = jnp.zeros((8 - top, block), jnp.float32)


def slot_pass(rows, meta, gate_weight, up_weight, down_weight):
    slots, width, units = gate_weight.shape
    block = rows.shape[2]
    tall = pl.BlockSpec((1, width, units), lambda s: (s, 0, 0))
    wide = pl.BlockSpec((1, units, width), lambda s: (s, 0, 0))
    whole = pl.BlockSpec(memory_space=pltpu.VMEM)
    row_shape = (slots, 4, MOST, width)
    back_shape = (4, slots, MOST, width)
    flops = 2 * 9 * slots * 4 * MOST * width * units
    return pl.pallas_call(
        slot_kernel,
        grid=(slots,),
        out_shape=(
            jax.ShapeDtypeStruct((slots, width, units), jnp.bfloat16),
            jax.ShapeDtypeStruct((slots, width, units), jnp.bfloat16),
            jax.ShapeDtypeStruct((slots, units, width), jnp.bfloat16),
            jax.ShapeDtypeStruct((4, 4, 2, block // 4, width), jnp.bfloat16),
            jax.ShapeDtypeStruct((4, 8, block), jnp.float32),
        ),
        in_specs=[whole, whole, tall, tall, wide],
        out_specs=[tall, tall, wide, whole, whole],
        scratch_shapes=[
            pltpu.VMEM(row_shape, jnp.bfloat16),
            pltpu.VMEM(row_shape, jnp.bfloat16),
            pltpu.VMEM(back_shape, jnp.bfloat16),
            pltpu.VMEM(back_shape, jnp.bfloat16),
            pltpu.VMEM((4, slots * MOST, block), jnp.bfloat16),
            pltpu.VMEM((slots, 4, MOST, 1), jnp.float32),
            pltpu.VMEM((slots, 4, MOST, 1), jnp.float32),
        ],
        compiler_params=pltpu.CompilerParams(vmem_limit_bytes=48 * 2**20),
        cost_estimate=pl.CostEstimate(
            flops=flops, bytes_accessed=12 * slots * width * units, transcendentals=0
        ),
    )(rows, meta, gate_weight, up_weight, down_weight)


def reduce_kernel(
    part_ref, prob_ref, layer_ref, token_ref, prob_out,
    near, crossing, crossed, summed, arrived, final, prob_in, prob_all, send, recv,
):
    e, r, core, across, diagonal = positions()
    quarter = part_ref.shape[3]
    greet(
        [place(expert=lax.rem(e + j, 4)) for j in (1, 2, 3)]
        + [place(replica=lax.rem(r + i, 4)) for i in (1, 2, 3)]
    )
    order = (2, 1, 3, 0)
    block = [lax.rem(e + j, 4) for j in range(4)]
    far, close, cross, along, back, forth, last = {}, {}, {}, {}, {}, {}, {}
    for j in order:
        far[j] = remote(
            part_ref.at[diagonal, block[j]], near.at[0, j], send.at[0, j], recv.at[0, j],
            place(replica=core),
        )
    for j in (1, 2, 3):
        back[j] = remote(
            prob_ref.at[block[j]], prob_in.at[j], send.at[1, j], recv.at[1, j],
            place(expert=block[j]),
        )
    for j in order:
        close[j] = remote(
            part_ref.at[core, block[j]], near.at[1, j], send.at[2, j], recv.at[2, j],
            place(replica=core),
        )

    def wide(value):
        return value.astype(jnp.float32)

    for j in order:
        far[j].wait_recv()
        crossing[j] = (wide(part_ref[across, block[j]]) + wide(near[0, j])).astype(jnp.bfloat16)
        cross[j] = remote(
            crossing.at[j], crossed.at[j], send.at[3, j], recv.at[3, j], place(replica=across)
        )
    for j in order:
        close[j].wait_recv()
        cross[j].wait_recv()
        total = wide(part_ref[r, block[j]]) + wide(near[1, j]) + wide(crossed[j])
        summed[j] = total.astype(jnp.bfloat16)
        if j > 0:
            along[j] = remote(
                summed.at[j], arrived.at[j], send.at[4, j], recv.at[4, j], place(expert=block[j])
            )
    for j in (1, 2, 3):
        back[j].wait_recv()
    prob_all[r] = prob_ref[e] + prob_in[1] + prob_in[2] + prob_in[3]
    for i in (1, 2, 3):
        forth[i] = remote(
            prob_all.at[r], prob_all.at[r], send.at[5, i], recv.at[5, i],
            place(replica=lax.rem(r + i, 4)),
        )
    for j in (1, 2, 3):
        along[j].wait_recv()
    final[r] = (
        wide(summed[0]) + wide(arrived[1]) + wide(arrived[2]) + wide(arrived[3])
    ).astype(jnp.bfloat16)
    own = final.at[r]
    last[0] = remote(own, own, send.at[6, 0], recv.at[6, 0], place(replica=across))
    last[1] = remote(own, own, send.at[6, 1], recv.at[6, 1], place(replica=core))
    for i in (1, 2, 3):
        forth[i].wait()
    prob_out[...] = prob_all[0] + prob_all[1] + prob_all[2] + prob_all[3]
    last[0].wait_recv()
    passed = final.at[across]
    last[2] = remote(passed, passed, send.at[6, 2], recv.at[6, 2], place(replica=core))
    last[1].wait_recv()
    last[2].wait_recv()
    for q in range(4):
        layer_ref[q * quarter : (q + 1) * quarter, :] = final[q, 0]
        token_ref[q * quarter : (q + 1) * quarter, :] = final[q, 1]
    for j in order:
        far[j].wait_send()
        close[j].wait_send()
        cross[j].wait_send()
        if j > 0:
            back[j].wait_send()
            along[j].wait_send()
    for i in range(3):
        last[i].wait_send()


def reduce_all(part, prob):
    quarter, width = part.shape[3:]
    block = 4 * quarter
    piece = (4, 2, quarter, width)
    return pl.pallas_call(
        reduce_kernel,
        out_shape=(
            jax.ShapeDtypeStruct((block, width), jnp.bfloat16),
            jax.ShapeDtypeStruct((block, width), jnp.bfloat16),
            jax.ShapeDtypeStruct((8, block), jnp.float32),
        ),
        in_specs=[pl.BlockSpec(memory_space=pltpu.VMEM)] * 2,
        out_specs=[pl.BlockSpec(memory_space=pltpu.VMEM)] * 3,
        scratch_shapes=[
            pltpu.VMEM((2,) + piece, jnp.bfloat16),
            pltpu.VMEM(piece, jnp.bfloat16),
            pltpu.VMEM(piece, jnp.bfloat16),
            pltpu.VMEM(piece, jnp.bfloat16),
            pltpu.VMEM(piece, jnp.bfloat16),
            pltpu.VMEM(piece, jnp.bfloat16),
            pltpu.VMEM((4, 8, block), jnp.float32),
            pltpu.VMEM((4, 8, block), jnp.float32),
            pltpu.SemaphoreType.DMA((7, 4)),
            pltpu.SemaphoreType.DMA((7, 4)),
        ],
        compiler_params=pltpu.CompilerParams(
            collective_id=1, has_side_effects=True, vmem_limit_bytes=24 * 2**20
        ),
    )(part, prob)


def gathered_shards(
    tokens, out_grad, route_probs, routes, placement, gate_weight, up_weight, down_weight
):
    block, top_k = routes.shape
    expert_ids = jnp.arange(placement.shape[0], dtype=jnp.int32)
    matches = routes.T[:, :, None] == expert_ids
    slot_ids = jnp.sum(jnp.where(matches, placement, 0), axis=2, dtype=jnp.int32)
    fill = ((0, 8 - top_k), (0, 0))
    meta = jnp.concatenate(
        [
            jnp.pad(slot_ids.astype(jnp.float32), fill, constant_values=-1.0),
            jnp.pad(route_probs.T, fill),
        ],
        axis=0,
    )
    rows, meta_all = gather_all(tokens, out_grad, meta)
    gate_grad, up_grad, down_grad, part, prob = slot_pass(
        rows, meta_all, gate_weight, up_weight, down_weight
    )
    layer_out, token_grad, prob_sum = reduce_all(part, prob)
    return (layer_out, token_grad, prob_sum[:top_k].T, gate_grad, up_grad, down_grad)


def solution(mesh):
    in_specs = (
        P(("groups", "expert"), None),
        P(("groups", "expert"), None),
        P(("groups", "expert"), None),
        P(("groups", "expert"), None),
        P(),
        P("expert", None, "replica"),
        P("expert", None, "replica"),
        P("expert", "replica", None),
    )
    out_specs = (
        P(("groups", "expert"), None),
        P(("groups", "expert"), None),
        P(("groups", "expert"), None),
        P(("groups", "expert"), None, "replica"),
        P(("groups", "expert"), None, "replica"),
        P(("groups", "expert"), "replica", None),
    )
    small = mesh.shape["expert"] == 4 and mesh.shape["replica"] == 4
    body = gathered_shards if small else shards
    return jax.shard_map(body, mesh=mesh, in_specs=in_specs, out_specs=out_specs, check_vma=False)
```

```python
import jax
import jax.numpy as jnp
from jax import lax
from jax.experimental import pallas as pl
from jax.experimental.pallas import tpu as pltpu
from jax.sharding import PartitionSpec as P

MOST = 16
MESH = pl.DeviceIdType.MESH


def expert_rows(input_rows, back_rows, gate_weight, up_weight, down_weight):
    gate_pre = jnp.einsum(
        "slcd,ldh->slch", input_rows, gate_weight, preferred_element_type=jnp.float32
    )
    up_pre = jnp.einsum("slcd,ldh->slch", input_rows, up_weight, preferred_element_type=jnp.float32)
    sigma_gate = jax.nn.sigmoid(gate_pre)
    swish_gate = gate_pre * sigma_gate
    hidden = (swish_gate * up_pre).astype(jnp.bfloat16)
    outputs = jnp.einsum("slch,lhd->slcd", hidden, down_weight, preferred_element_type=jnp.float32)
    hidden_grad = jnp.einsum(
        "slcd,lhd->slch", back_rows, down_weight, preferred_element_type=jnp.float32
    )
    gate_back = (hidden_grad * up_pre * sigma_gate * (1.0 + gate_pre * (1.0 - sigma_gate))).astype(
        jnp.bfloat16
    )
    up_back = (hidden_grad * swish_gate).astype(jnp.bfloat16)
    input_grad = jnp.einsum(
        "slch,ldh->slcd", gate_back, gate_weight, preferred_element_type=jnp.float32
    )
    input_grad = input_grad + jnp.einsum(
        "slch,ldh->slcd", up_back, up_weight, preferred_element_type=jnp.float32
    )
    return (outputs, input_grad, hidden, gate_back, up_back)


def shards(tokens, out_grad, route_probs, routes, placement, gate_weight, up_weight, down_weight):
    local_experts = gate_weight.shape[0]
    index_count = lax.axis_size("expert")
    experts_all = placement.shape[0]
    tok_rows, top_k = routes.shape
    model_width = tokens.shape[1]
    capacity = MOST
    expert_ids = jnp.arange(experts_all, dtype=jnp.int32)
    match_table = routes.reshape(-1)[:, None] == expert_ids[None, :]
    slot_ids = jnp.sum(jnp.where(match_table, placement[None, :], 0), axis=1, dtype=jnp.int32)
    slot_match = (slot_ids[:, None] == expert_ids[None, :]).astype(jnp.int32)
    rank_ids = jnp.sum(
        (jnp.cumsum(slot_match, axis=0, dtype=jnp.int32) - 1) * slot_match, axis=1, dtype=jnp.int32
    )
    position = slot_ids * capacity + rank_ids
    route_count = tok_rows * top_k
    buffer_rows = experts_all * capacity
    route_of = (
        jnp.full((buffer_rows,), route_count, jnp.int32)
        .at[position]
        .set(jnp.arange(route_count, dtype=jnp.int32))
    )
    filled = route_of < route_count
    safe_route = jnp.where(filled, route_of, 0)
    token_of = safe_route // top_k
    probs_flat = route_probs.reshape(-1)
    input_send = jnp.where(filled[:, None], tokens[token_of], jnp.zeros((), jnp.bfloat16))
    scaled = probs_flat[safe_route][:, None] * out_grad[token_of].astype(jnp.float32)
    back_send = jnp.where(filled[:, None], scaled, 0.0).astype(jnp.bfloat16)
    buffer_shape = (index_count, local_experts, capacity, model_width)
    input_send = input_send.reshape(buffer_shape)
    back_send = back_send.reshape(buffer_shape)
    input_piece = lax.all_to_all(input_send, "expert", split_axis=0, concat_axis=0, tiled=True)
    back_piece = lax.all_to_all(back_send, "expert", split_axis=0, concat_axis=0, tiled=True)
    results = expert_rows(input_piece, back_piece, gate_weight, up_weight, down_weight)
    input_rows, back_rows, outputs, input_grad, hidden, gate_back, up_back = (
        input_piece,
        back_piece,
    ) + results
    gate_grad = jnp.einsum(
        "slcd,slch->ldh", input_rows, gate_back, preferred_element_type=jnp.float32
    ).astype(jnp.bfloat16)
    up_grad = jnp.einsum(
        "slcd,slch->ldh", input_rows, up_back, preferred_element_type=jnp.float32
    ).astype(jnp.bfloat16)
    down_grad = jnp.einsum(
        "slch,slcd->lhd", hidden, back_rows, preferred_element_type=jnp.float32
    ).astype(jnp.bfloat16)
    out_back, grad_back = (
        lax.all_to_all(
            outputs.astype(jnp.bfloat16), "expert", split_axis=0, concat_axis=0, tiled=True
        ),
        lax.all_to_all(
            input_grad.astype(jnp.bfloat16), "expert", split_axis=0, concat_axis=0, tiled=True
        ),
    )
    kept_mask = rank_ids >= 0
    out_rows = out_back.reshape(-1, model_width)[position].astype(jnp.float32)
    grad_rows = grad_back.reshape(-1, model_width)[position].astype(jnp.float32)
    kept_rows = kept_mask.reshape(tok_rows, top_k)
    route_weight = jnp.where(kept_mask, probs_flat, 0.0).reshape(tok_rows, top_k)
    out_rows = out_rows.reshape(tok_rows, top_k, model_width)
    grad_rows = grad_rows.reshape(tok_rows, top_k, model_width)
    layer_part = jnp.sum(route_weight[:, :, None] * out_rows, axis=1)
    token_part = jnp.sum(jnp.where(kept_rows[:, :, None], grad_rows, 0.0), axis=1)
    prob_part = jnp.where(
        kept_rows, jnp.sum(out_grad.astype(jnp.float32)[:, None, :] * out_rows, axis=2), 0.0
    )
    layer_sum, token_sum, prob_sum = (
        lax.psum(layer_part.astype(jnp.bfloat16), "replica").astype(jnp.float32),
        lax.psum(token_part.astype(jnp.bfloat16), "replica").astype(jnp.float32),
        lax.psum(prob_part.astype(jnp.bfloat16), "replica").astype(jnp.float32),
    )
    return (
        layer_sum.astype(jnp.bfloat16),
        token_sum.astype(jnp.bfloat16),
        prob_sum,
        gate_grad,
        up_grad,
        down_grad,
    )


def place(expert=None, replica=None):
    own = [lax.axis_index("groups"), lax.axis_index("expert"), lax.axis_index("replica")]
    if expert is not None:
        own[1] = expert
    if replica is not None:
        own[2] = replica
    return tuple(own)


def greet(devices):
    barrier = pltpu.get_barrier_semaphore()
    for device in devices:
        pl.semaphore_signal(barrier, inc=1, device_id=device, device_id_type=MESH)
    pl.semaphore_wait(barrier, len(devices))


def positions():
    e, r = lax.axis_index("expert"), lax.axis_index("replica")
    core = r + 1 - 2 * lax.rem(r, 2)
    across = lax.rem(r + 2, 4)
    diagonal = lax.rem(core + 2, 4)
    return e, r, core, across, diagonal


def remote(src, dst, send, recv, device):
    copy = pltpu.make_async_remote_copy(
        src_ref=src, dst_ref=dst, send_sem=send, recv_sem=recv, device_id=device, device_id_type=MESH
    )
    copy.start()
    return copy


def gather_kernel(x_ref, g_ref, m_ref, rows_ref, meta_ref, send, recv):
    e, r, core, across, _ = positions()
    quarter = x_ref.shape[0] // 4
    greet(
        [place(expert=lax.rem(e + j, 4)) for j in (1, 2, 3)]
        + [place(replica=core), place(replica=across)]
    )
    rows_ref[e, 0] = x_ref[...]
    rows_ref[e, 1] = g_ref[...]
    meta_ref[e] = m_ref[...]
    mine = pl.ds(pl.multiple_of(r * quarter, quarter), quarter)
    other = pl.ds(pl.multiple_of(across * quarter, quarter), quarter)
    first, metas = {}, {}
    for j in (2, 1, 3):
        peer = place(expert=lax.rem(e + j, 4))
        own = rows_ref.at[e, :, mine]
        metas[j] = remote(meta_ref.at[e], meta_ref.at[e], send.at[0, j], recv.at[0, j], peer)
        first[j] = remote(own, own, send.at[1, j], recv.at[1, j], peer)
    passed, spread, last = {}, {}, {}
    for j in (1, 3, 2):
        block = lax.rem(e + 4 - j, 4)
        first[j].wait_recv()
        part = rows_ref.at[block, :, mine]
        passed[j] = remote(part, part, send.at[2, j], recv.at[2, j], place(replica=across))
        spread[j] = remote(part, part, send.at[3, j], recv.at[3, j], place(replica=core))
    for j in (1, 3, 2):
        block = lax.rem(e + 4 - j, 4)
        passed[j].wait_recv()
        part = rows_ref.at[block, :, other]
        last[j] = remote(part, part, send.at[4, j], recv.at[4, j], place(replica=core))
    for j in (1, 3, 2):
        metas[j].wait()
        first[j].wait_send()
        passed[j].wait_send()
        spread[j].wait()
        last[j].wait()


def gather_all(tokens, out_grad, meta):
    block, width = tokens.shape
    return pl.pallas_call(
        gather_kernel,
        out_shape=(
            jax.ShapeDtypeStruct((4, 2, block, width), jnp.bfloat16),
            jax.ShapeDtypeStruct((4,) + meta.shape, jnp.float32),
        ),
        in_specs=[pl.BlockSpec(memory_space=pltpu.VMEM)] * 3,
        out_specs=[pl.BlockSpec(memory_space=pltpu.VMEM)] * 2,
        scratch_shapes=[pltpu.SemaphoreType.DMA((5, 4)), pltpu.SemaphoreType.DMA((5, 4))],
        compiler_params=pltpu.CompilerParams(
            collective_id=0, has_side_effects=True, vmem_limit_bytes=24 * 2**20
        ),
    )(tokens, out_grad, meta)


def dot(left, right, left_dim, right_dim):
    return lax.dot_general(
        left, right, (((left_dim,), (right_dim,)), ((), ())), preferred_element_type=jnp.float32
    )


def slot_kernel(
    rows_ref, meta_ref, gate_ref, up_ref, down_ref,
    gate_out, up_out, down_out, part_ref, prob_ref,
    x_rows, g_rows, out_rows, grad_rows, pick_ref, weight_ref, inner_ref,
):
    s = pl.program_id(0)
    slots = pl.num_programs(0)
    block = rows_ref.shape[2]
    width = rows_ref.shape[3]
    top = 6
    held = slots * MOST
    base = lax.axis_index("expert") * slots

    def slot_names():
        names = lax.broadcasted_iota(jnp.int32, (slots, block), 0) + base
        return names.astype(jnp.float32)

    @pl.when(s == 0)
    def _():
        names = slot_names()
        before = lax.broadcasted_iota(jnp.int32, (block, block), 0)
        after = lax.broadcasted_iota(jnp.int32, (block, block), 1)
        earlier = (before < after).astype(jnp.float32).astype(jnp.bfloat16)
        ranks = lax.broadcasted_iota(jnp.int32, (slots, MOST, block), 1).astype(jnp.float32)
        for b in range(4):
            named = jnp.zeros((slots, block), jnp.float32)
            probs = jnp.zeros((slots, block), jnp.float32)
            for k in range(top):
                same = meta_ref[b, k : k + 1, :] == names
                named = named + jnp.where(same, 1.0, 0.0)
                probs = probs + jnp.where(same, meta_ref[b, 8 + k : 9 + k, :], 0.0)
            rank = dot(named.astype(jnp.bfloat16), earlier, 1, 0)
            rank = jnp.where(named > 0.0, rank, -1.0)
            pick = jnp.where(rank[:, None, :] == ranks, 1.0, 0.0)
            weight_ref[:, b] = jnp.sum(pick * probs[:, None, :], axis=2, keepdims=True)
            chosen = pick.reshape(held, block).astype(jnp.bfloat16)
            pick_ref[b] = chosen
            x_rows[:, b] = (
                dot(chosen, rows_ref[b, 0], 1, 0).astype(jnp.bfloat16).reshape(slots, MOST, width)
            )
            g_rows[:, b] = (
                dot(chosen, rows_ref[b, 1], 1, 0).astype(jnp.bfloat16).reshape(slots, MOST, width)
            )

    x = x_rows[s].reshape(4 * MOST, width)
    g = g_rows[s].reshape(4 * MOST, width)
    weight = weight_ref[s].reshape(4 * MOST, 1)
    gate_w, up_w, down_w = gate_ref[0], up_ref[0], down_ref[0]
    gate_pre = dot(x, gate_w, 1, 1)
    up_pre = dot(x, up_w, 1, 1)
    plain_grad = dot(g, down_w, 1, 1)
    sigma = jax.nn.sigmoid(gate_pre)
    swish = gate_pre * sigma
    hidden = (swish * up_pre).astype(jnp.bfloat16).astype(jnp.float32)
    inner = jnp.sum(hidden * plain_grad, axis=1, keepdims=True)
    inner_ref[s] = inner.reshape(4, MOST, 1)
    hidden_grad = plain_grad * weight
    gate_back = (hidden_grad * up_pre * sigma * (1.0 + gate_pre * (1.0 - sigma))).astype(
        jnp.bfloat16
    )
    up_back = (hidden_grad * swish).astype(jnp.bfloat16)
    scaled = (hidden * weight).astype(jnp.bfloat16)
    output = dot(scaled, down_w, 1, 0).astype(jnp.bfloat16).reshape(4, MOST, width)
    input_grad = dot(gate_back, gate_w, 1, 0) + dot(up_back, up_w, 1, 0)
    input_grad = input_grad.astype(jnp.bfloat16).reshape(4, MOST, width)
    for b in range(4):
        out_rows[b, s] = output[b]
        grad_rows[b, s] = input_grad[b]
    gate_out[0] = dot(gate_back, x, 0, 0).astype(jnp.bfloat16)
    up_out[0] = dot(up_back, x, 0, 0).astype(jnp.bfloat16)
    down_out[0] = dot(scaled, g, 0, 0).astype(jnp.bfloat16)

    @pl.when(s == slots - 1)
    def _():
        names = slot_names()
        quarter = block // 4
        for b in range(4):
            chosen = pick_ref[b]
            for a, held_rows in ((0, out_rows), (1, grad_rows)):
                total = dot(chosen, held_rows[b].reshape(held, width), 0, 0).astype(jnp.bfloat16)
                for q in range(4):
                    part_ref[q, b, a] = total[q * quarter : (q + 1) * quarter]
            pick = chosen.astype(jnp.float32).reshape(slots, MOST, block)
            inner_of = jnp.sum(pick * inner_ref[:, b], axis=1)
            for k in range(top):
                same = meta_ref[b, k : k + 1, :] == names
                prob_ref[b, k : k + 1, :] = jnp.sum(
                    jnp.where(same, inner_of, 0.0), axis=0, keepdims=True
                )
            prob_ref[b, top:8, :] = jnp.zeros((8 - top, block), jnp.float32)


def slot_pass(rows, meta, gate_weight, up_weight, down_weight):
    slots, units, width = gate_weight.shape
    block = rows.shape[2]
    wide = pl.BlockSpec((1, units, width), lambda s: (s, 0, 0))
    whole = pl.BlockSpec(memory_space=pltpu.VMEM)
    row_shape = (slots, 4, MOST, width)
    back_shape = (4, slots, MOST, width)
    flops = 2 * 9 * slots * 4 * MOST * width * units
    return pl.pallas_call(
        slot_kernel,
        grid=(slots,),
        out_shape=(
            jax.ShapeDtypeStruct((slots, units, width), jnp.bfloat16),
            jax.ShapeDtypeStruct((slots, units, width), jnp.bfloat16),
            jax.ShapeDtypeStruct((slots, units, width), jnp.bfloat16),
            jax.ShapeDtypeStruct((4, 4, 2, block // 4, width), jnp.bfloat16),
            jax.ShapeDtypeStruct((4, 8, block), jnp.float32),
        ),
        in_specs=[whole, whole, wide, wide, wide],
        out_specs=[wide, wide, wide, whole, whole],
        scratch_shapes=[
            pltpu.VMEM(row_shape, jnp.bfloat16),
            pltpu.VMEM(row_shape, jnp.bfloat16),
            pltpu.VMEM(back_shape, jnp.bfloat16),
            pltpu.VMEM(back_shape, jnp.bfloat16),
            pltpu.VMEM((4, slots * MOST, block), jnp.bfloat16),
            pltpu.VMEM((slots, 4, MOST, 1), jnp.float32),
            pltpu.VMEM((slots, 4, MOST, 1), jnp.float32),
        ],
        compiler_params=pltpu.CompilerParams(vmem_limit_bytes=48 * 2**20),
        cost_estimate=pl.CostEstimate(
            flops=flops, bytes_accessed=12 * slots * width * units, transcendentals=0
        ),
    )(rows, meta, gate_weight, up_weight, down_weight)


def reduce_kernel(
    part_ref, prob_ref, layer_ref, token_ref, prob_out,
    near, crossing, crossed, summed, arrived, final, prob_in, prob_all, send, recv,
):
    e, r, core, across, diagonal = positions()
    quarter = part_ref.shape[3]
    greet(
        [place(expert=lax.rem(e + j, 4)) for j in (1, 2, 3)]
        + [place(replica=lax.rem(r + i, 4)) for i in (1, 2, 3)]
    )
    order = (2, 1, 3, 0)
    block = [lax.rem(e + j, 4) for j in range(4)]
    far, close, cross, along, back, forth, last = {}, {}, {}, {}, {}, {}, {}
    for j in order:
        far[j] = remote(
            part_ref.at[diagonal, block[j]], near.at[0, j], send.at[0, j], recv.at[0, j],
            place(replica=core),
        )
    for j in (1, 2, 3):
        back[j] = remote(
            prob_ref.at[block[j]], prob_in.at[j], send.at[1, j], recv.at[1, j],
            place(expert=block[j]),
        )
    for j in order:
        close[j] = remote(
            part_ref.at[core, block[j]], near.at[1, j], send.at[2, j], recv.at[2, j],
            place(replica=core),
        )

    def wide(value):
        return value.astype(jnp.float32)

    for j in order:
        far[j].wait_recv()
        crossing[j] = (wide(part_ref[across, block[j]]) + wide(near[0, j])).astype(jnp.bfloat16)
        cross[j] = remote(
            crossing.at[j], crossed.at[j], send.at[3, j], recv.at[3, j], place(replica=across)
        )
    for j in order:
        close[j].wait_recv()
        cross[j].wait_recv()
        total = wide(part_ref[r, block[j]]) + wide(near[1, j]) + wide(crossed[j])
        summed[j] = total.astype(jnp.bfloat16)
        if j > 0:
            along[j] = remote(
                summed.at[j], arrived.at[j], send.at[4, j], recv.at[4, j], place(expert=block[j])
            )
    for j in (1, 2, 3):
        back[j].wait_recv()
    prob_all[r] = prob_ref[e] + prob_in[1] + prob_in[2] + prob_in[3]
    for i in (1, 2, 3):
        forth[i] = remote(
            prob_all.at[r], prob_all.at[r], send.at[5, i], recv.at[5, i],
            place(replica=lax.rem(r + i, 4)),
        )
    for j in (1, 2, 3):
        along[j].wait_recv()
    final[r] = (
        wide(summed[0]) + wide(arrived[1]) + wide(arrived[2]) + wide(arrived[3])
    ).astype(jnp.bfloat16)
    own = final.at[r]
    last[0] = remote(own, own, send.at[6, 0], recv.at[6, 0], place(replica=across))
    last[1] = remote(own, own, send.at[6, 1], recv.at[6, 1], place(replica=core))
    for i in (1, 2, 3):
        forth[i].wait()
    prob_out[...] = prob_all[0] + prob_all[1] + prob_all[2] + prob_all[3]
    last[0].wait_recv()
    passed = final.at[across]
    last[2] = remote(passed, passed, send.at[6, 2], recv.at[6, 2], place(replica=core))
    last[1].wait_recv()
    last[2].wait_recv()
    for q in range(4):
        layer_ref[q * quarter : (q + 1) * quarter, :] = final[q, 0]
        token_ref[q * quarter : (q + 1) * quarter, :] = final[q, 1]
    for j in order:
        far[j].wait_send()
        close[j].wait_send()
        cross[j].wait_send()
        if j > 0:
            back[j].wait_send()
            along[j].wait_send()
    for i in range(3):
        last[i].wait_send()


def reduce_all(part, prob):
    quarter, width = part.shape[3:]
    block = 4 * quarter
    piece = (4, 2, quarter, width)
    return pl.pallas_call(
        reduce_kernel,
        out_shape=(
            jax.ShapeDtypeStruct((block, width), jnp.bfloat16),
            jax.ShapeDtypeStruct((block, width), jnp.bfloat16),
            jax.ShapeDtypeStruct((8, block), jnp.float32),
        ),
        in_specs=[pl.BlockSpec(memory_space=pltpu.VMEM)] * 2,
        out_specs=[pl.BlockSpec(memory_space=pltpu.VMEM)] * 3,
        scratch_shapes=[
            pltpu.VMEM((2,) + piece, jnp.bfloat16),
            pltpu.VMEM(piece, jnp.bfloat16),
            pltpu.VMEM(piece, jnp.bfloat16),
            pltpu.VMEM(piece, jnp.bfloat16),
            pltpu.VMEM(piece, jnp.bfloat16),
            pltpu.VMEM(piece, jnp.bfloat16),
            pltpu.VMEM((4, 8, block), jnp.float32),
            pltpu.VMEM((4, 8, block), jnp.float32),
            pltpu.SemaphoreType.DMA((7, 4)),
            pltpu.SemaphoreType.DMA((7, 4)),
        ],
        compiler_params=pltpu.CompilerParams(
            collective_id=1, has_side_effects=True, vmem_limit_bytes=24 * 2**20
        ),
    )(part, prob)


def gathered_shards(
    tokens, out_grad, route_probs, routes, placement, gate_weight, up_weight, down_weight
):
    block, top_k = routes.shape
    expert_ids = jnp.arange(placement.shape[0], dtype=jnp.int32)
    matches = routes.T[:, :, None] == expert_ids
    slot_ids = jnp.sum(jnp.where(matches, placement, 0), axis=2, dtype=jnp.int32)
    fill = ((0, 8 - top_k), (0, 0))
    meta = jnp.concatenate(
        [
            jnp.pad(slot_ids.astype(jnp.float32), fill, constant_values=-1.0),
            jnp.pad(route_probs.T, fill),
        ],
        axis=0,
    )
    rows, meta_all = gather_all(tokens, out_grad, meta)
    gate_grad, up_grad, down_grad, part, prob = slot_pass(
        rows, meta_all, jnp.swapaxes(gate_weight, 1, 2), jnp.swapaxes(up_weight, 1, 2), down_weight
    )
    gate_grad, up_grad = jnp.swapaxes(gate_grad, 1, 2), jnp.swapaxes(up_grad, 1, 2)
    layer_out, token_grad, prob_sum = reduce_all(part, prob)
    return (layer_out, token_grad, prob_sum[:top_k].T, gate_grad, up_grad, down_grad)


def solution(mesh):
    in_specs = (
        P(("groups", "expert"), None),
        P(("groups", "expert"), None),
        P(("groups", "expert"), None),
        P(("groups", "expert"), None),
        P(),
        P("expert", None, "replica"),
        P("expert", None, "replica"),
        P("expert", "replica", None),
    )
    out_specs = (
        P(("groups", "expert"), None),
        P(("groups", "expert"), None),
        P(("groups", "expert"), None),
        P(("groups", "expert"), None, "replica"),
        P(("groups", "expert"), None, "replica"),
        P(("groups", "expert"), "replica", None),
    )
    small = mesh.shape["expert"] == 4 and mesh.shape["replica"] == 4
    body = gathered_shards if small else shards
    return jax.shard_map(body, mesh=mesh, in_specs=in_specs, out_specs=out_specs, check_vma=False)
```

```python
import jax
import jax.numpy as jnp
from jax import lax
from jax.experimental import pallas as pl
from jax.experimental.pallas import tpu as pltpu
from jax.sharding import PartitionSpec as P

MOST = 16
MESH = pl.DeviceIdType.MESH


def expert_rows(input_rows, back_rows, gate_weight, up_weight, down_weight):
    gate_pre = jnp.einsum(
        "slcd,ldh->slch", input_rows, gate_weight, preferred_element_type=jnp.float32
    )
    up_pre = jnp.einsum("slcd,ldh->slch", input_rows, up_weight, preferred_element_type=jnp.float32)
    sigma_gate = jax.nn.sigmoid(gate_pre)
    swish_gate = gate_pre * sigma_gate
    hidden = (swish_gate * up_pre).astype(jnp.bfloat16)
    outputs = jnp.einsum("slch,lhd->slcd", hidden, down_weight, preferred_element_type=jnp.float32)
    hidden_grad = jnp.einsum(
        "slcd,lhd->slch", back_rows, down_weight, preferred_element_type=jnp.float32
    )
    gate_back = (hidden_grad * up_pre * sigma_gate * (1.0 + gate_pre * (1.0 - sigma_gate))).astype(
        jnp.bfloat16
    )
    up_back = (hidden_grad * swish_gate).astype(jnp.bfloat16)
    input_grad = jnp.einsum(
        "slch,ldh->slcd", gate_back, gate_weight, preferred_element_type=jnp.float32
    )
    input_grad = input_grad + jnp.einsum(
        "slch,ldh->slcd", up_back, up_weight, preferred_element_type=jnp.float32
    )
    return (outputs, input_grad, hidden, gate_back, up_back)


def shards(tokens, out_grad, route_probs, routes, placement, gate_weight, up_weight, down_weight):
    local_experts = gate_weight.shape[0]
    index_count = lax.axis_size("expert")
    experts_all = placement.shape[0]
    tok_rows, top_k = routes.shape
    model_width = tokens.shape[1]
    capacity = MOST
    expert_ids = jnp.arange(experts_all, dtype=jnp.int32)
    match_table = routes.reshape(-1)[:, None] == expert_ids[None, :]
    slot_ids = jnp.sum(jnp.where(match_table, placement[None, :], 0), axis=1, dtype=jnp.int32)
    slot_match = (slot_ids[:, None] == expert_ids[None, :]).astype(jnp.int32)
    rank_ids = jnp.sum(
        (jnp.cumsum(slot_match, axis=0, dtype=jnp.int32) - 1) * slot_match, axis=1, dtype=jnp.int32
    )
    position = slot_ids * capacity + rank_ids
    route_count = tok_rows * top_k
    buffer_rows = experts_all * capacity
    route_of = (
        jnp.full((buffer_rows,), route_count, jnp.int32)
        .at[position]
        .set(jnp.arange(route_count, dtype=jnp.int32))
    )
    filled = route_of < route_count
    safe_route = jnp.where(filled, route_of, 0)
    token_of = safe_route // top_k
    probs_flat = route_probs.reshape(-1)
    input_send = jnp.where(filled[:, None], tokens[token_of], jnp.zeros((), jnp.bfloat16))
    scaled = probs_flat[safe_route][:, None] * out_grad[token_of].astype(jnp.float32)
    back_send = jnp.where(filled[:, None], scaled, 0.0).astype(jnp.bfloat16)
    buffer_shape = (index_count, local_experts, capacity, model_width)
    input_send = input_send.reshape(buffer_shape)
    back_send = back_send.reshape(buffer_shape)
    input_piece = lax.all_to_all(input_send, "expert", split_axis=0, concat_axis=0, tiled=True)
    back_piece = lax.all_to_all(back_send, "expert", split_axis=0, concat_axis=0, tiled=True)
    results = expert_rows(input_piece, back_piece, gate_weight, up_weight, down_weight)
    input_rows, back_rows, outputs, input_grad, hidden, gate_back, up_back = (
        input_piece,
        back_piece,
    ) + results
    gate_grad = jnp.einsum(
        "slcd,slch->ldh", input_rows, gate_back, preferred_element_type=jnp.float32
    ).astype(jnp.bfloat16)
    up_grad = jnp.einsum(
        "slcd,slch->ldh", input_rows, up_back, preferred_element_type=jnp.float32
    ).astype(jnp.bfloat16)
    down_grad = jnp.einsum(
        "slch,slcd->lhd", hidden, back_rows, preferred_element_type=jnp.float32
    ).astype(jnp.bfloat16)
    out_back, grad_back = (
        lax.all_to_all(
            outputs.astype(jnp.bfloat16), "expert", split_axis=0, concat_axis=0, tiled=True
        ),
        lax.all_to_all(
            input_grad.astype(jnp.bfloat16), "expert", split_axis=0, concat_axis=0, tiled=True
        ),
    )
    kept_mask = rank_ids >= 0
    out_rows = out_back.reshape(-1, model_width)[position].astype(jnp.float32)
    grad_rows = grad_back.reshape(-1, model_width)[position].astype(jnp.float32)
    kept_rows = kept_mask.reshape(tok_rows, top_k)
    route_weight = jnp.where(kept_mask, probs_flat, 0.0).reshape(tok_rows, top_k)
    out_rows = out_rows.reshape(tok_rows, top_k, model_width)
    grad_rows = grad_rows.reshape(tok_rows, top_k, model_width)
    layer_part = jnp.sum(route_weight[:, :, None] * out_rows, axis=1)
    token_part = jnp.sum(jnp.where(kept_rows[:, :, None], grad_rows, 0.0), axis=1)
    prob_part = jnp.where(
        kept_rows, jnp.sum(out_grad.astype(jnp.float32)[:, None, :] * out_rows, axis=2), 0.0
    )
    layer_sum, token_sum, prob_sum = (
        lax.psum(layer_part.astype(jnp.bfloat16), "replica").astype(jnp.float32),
        lax.psum(token_part.astype(jnp.bfloat16), "replica").astype(jnp.float32),
        lax.psum(prob_part.astype(jnp.bfloat16), "replica").astype(jnp.float32),
    )
    return (
        layer_sum.astype(jnp.bfloat16),
        token_sum.astype(jnp.bfloat16),
        prob_sum,
        gate_grad,
        up_grad,
        down_grad,
    )


def place(expert=None, replica=None):
    own = [lax.axis_index("groups"), lax.axis_index("expert"), lax.axis_index("replica")]
    if expert is not None:
        own[1] = expert
    if replica is not None:
        own[2] = replica
    return tuple(own)


def greet(devices):
    barrier = pltpu.get_barrier_semaphore()
    for device in devices:
        pl.semaphore_signal(barrier, inc=1, device_id=device, device_id_type=MESH)
    pl.semaphore_wait(barrier, len(devices))


def positions():
    e, r = lax.axis_index("expert"), lax.axis_index("replica")
    core = r + 1 - 2 * lax.rem(r, 2)
    across = lax.rem(r + 2, 4)
    diagonal = lax.rem(core + 2, 4)
    return e, r, core, across, diagonal


def remote(src, dst, send, recv, device):
    copy = pltpu.make_async_remote_copy(
        src_ref=src, dst_ref=dst, send_sem=send, recv_sem=recv, device_id=device, device_id_type=MESH
    )
    copy.start()
    return copy


def dot(left, right, left_dim, right_dim):
    return lax.dot_general(
        left, right, (((left_dim,), (right_dim,)), ((), ())), preferred_element_type=jnp.float32
    )

def route_kernel(
    x_ref, g_ref, m_ref, gate_hbm, up_hbm, down_hbm,
    layer_ref, token_ref, prob_out, x_rows, g_rows, scaled_ref, gate_back_ref, up_back_ref,
    rows_ref, meta_ref, gate_ref, up_ref, down_ref, gate_pre_ref, up_pre_ref, back_rows,
    pick_ref, weight_ref, inner_ref, part_ref, near, crossing, crossed, summed, arrived, final,
    prob_ref, prob_in, prob_all, load, send, recv, add_send, add_recv, prob_send, prob_recv,
):
    e, r, core, across, diagonal = positions()
    slots, units, width = gate_ref.shape
    block = x_ref.shape[0]
    quarter = block // 4
    top = 6
    held = slots * MOST
    rows = 4 * MOST
    mine = pl.ds(pl.multiple_of(r * quarter, quarter), quarter)
    other = pl.ds(pl.multiple_of(across * quarter, quarter), quarter)
    weights = ((gate_hbm, gate_ref), (up_hbm, up_ref), (down_hbm, down_ref))

    def fetch(s, start):
        for i, (source, target) in enumerate(weights):
            copy = pltpu.make_async_copy(source.at[s], target.at[s], load.at[i, s])
            if start:
                copy.start()
            else:
                copy.wait()

    def start_fetch(s, carry):
        fetch(s, True)
        return carry

    lax.fori_loop(0, slots, start_fetch, 0)
    rows_ref[0, e] = x_ref[...]
    rows_ref[1, e] = g_ref[...]
    meta_ref[e] = m_ref[...]
    greet(
        [place(expert=lax.rem(e + j, 4)) for j in (1, 2, 3)]
        + [place(replica=lax.rem(r + i, 4)) for i in (1, 2, 3)]
    )
    metas, first, passed, spread, last = {}, {}, {}, {}, {}
    for j in (2, 1, 3):
        peer = place(expert=lax.rem(e + j, 4))
        metas[j] = remote(meta_ref.at[e], meta_ref.at[e], send.at[0, 0, j], recv.at[0, 0, j], peer)
    for a in (0, 1):
        for j in (2, 1, 3):
            peer = place(expert=lax.rem(e + j, 4))
            own = rows_ref.at[a, e, mine]
            first[a, j] = remote(own, own, send.at[a, 1, j], recv.at[a, 1, j], peer)

    def pass_on(a):
        for j in (1, 3, 2):
            first[a, j].wait_recv()
            part = rows_ref.at[a, lax.rem(e + 4 - j, 4), mine]
            passed[a, j] = remote(
                part, part, send.at[a, 2, j], recv.at[a, 2, j], place(replica=across)
            )
            spread[a, j] = remote(
                part, part, send.at[a, 3, j], recv.at[a, 3, j], place(replica=core)
            )

    def pass_last(a):
        for j in (1, 3, 2):
            passed[a, j].wait_recv()
            part = rows_ref.at[a, lax.rem(e + 4 - j, 4), other]
            last[a, j] = remote(part, part, send.at[a, 4, j], recv.at[a, 4, j], place(replica=core))

    def received(a):
        for j in (1, 3, 2):
            spread[a, j].wait_recv()
            last[a, j].wait_recv()

    def slot_names():
        names = lax.broadcasted_iota(jnp.int32, (slots, block), 0) + e * slots
        return names.astype(jnp.float32)

    def wide(value):
        return value.astype(jnp.float32)

    def choose():
        names = slot_names()
        before = lax.broadcasted_iota(jnp.int32, (block, block), 0)
        after = lax.broadcasted_iota(jnp.int32, (block, block), 1)
        earlier = (before < after).astype(jnp.float32).astype(jnp.bfloat16)
        ranks = lax.broadcasted_iota(jnp.int32, (slots, MOST, block), 1).astype(jnp.float32)
        for b in range(4):
            named = jnp.zeros((slots, block), jnp.float32)
            probs = jnp.zeros((slots, block), jnp.float32)
            for k in range(top):
                same = meta_ref[b, k : k + 1, :] == names
                named = named + jnp.where(same, 1.0, 0.0)
                probs = probs + jnp.where(same, meta_ref[b, 8 + k : 9 + k, :], 0.0)
            rank = dot(named.astype(jnp.bfloat16), earlier, 1, 0)
            rank = jnp.where(named > 0.0, rank, -1.0)
            pick = jnp.where(rank[:, None, :] == ranks, 1.0, 0.0)
            weight_ref[:, b] = jnp.sum(pick * probs[:, None, :], axis=2, keepdims=True)
            pick_ref[b] = pick.reshape(held, block).astype(jnp.bfloat16)

    def take(a, target):
        for b in range(4):
            target[:, b] = (
                dot(pick_ref[b], rows_ref[a, b], 1, 0)
                .astype(jnp.bfloat16)
                .reshape(slots, MOST, width)
            )

    def keep(s, value):
        value = value.astype(jnp.bfloat16).reshape(4, MOST, width)
        for b in range(4):
            back_rows[b, s] = value[b]

    def forward(s, carry):
        fetch(s, False)
        x = x_rows[s].reshape(rows, width)
        gate_pre = dot(x, gate_ref[s], 1, 1)
        up_pre = dot(x, up_ref[s], 1, 1)
        gate_pre_ref[s] = gate_pre
        up_pre_ref[s] = up_pre
        hidden = wide((gate_pre * jax.nn.sigmoid(gate_pre) * up_pre).astype(jnp.bfloat16))
        scaled = (hidden * weight_ref[s].reshape(rows, 1)).astype(jnp.bfloat16)
        scaled_ref[s] = scaled
        keep(s, dot(scaled, down_ref[s], 1, 0))
        return carry

    def backward(s, carry):
        g = g_rows[s].reshape(rows, width)
        gate_pre, up_pre = gate_pre_ref[s], up_pre_ref[s]
        plain_grad = dot(g, down_ref[s], 1, 1)
        sigma = jax.nn.sigmoid(gate_pre)
        swish = gate_pre * sigma
        hidden = wide((swish * up_pre).astype(jnp.bfloat16))
        inner = jnp.sum(hidden * plain_grad, axis=1, keepdims=True)
        inner_ref[s] = inner.reshape(4, MOST, 1)
        hidden_grad = plain_grad * weight_ref[s].reshape(rows, 1)
        gate_back = (hidden_grad * up_pre * sigma * (1.0 + gate_pre * (1.0 - sigma))).astype(
            jnp.bfloat16
        )
        up_back = (hidden_grad * swish).astype(jnp.bfloat16)
        gate_back_ref[s] = gate_back
        up_back_ref[s] = up_back
        keep(s, dot(gate_back, gate_ref[s], 1, 0) + dot(up_back, up_ref[s], 1, 0))
        return carry

    order = (2, 1, 3, 0)
    where = [lax.rem(e + j, 4) for j in range(4)]
    far, close, cross, along, end = {}, {}, {}, {}, {}

    def gather_back(a):
        for j in order:
            total = dot(pick_ref[where[j]], back_rows[where[j]].reshape(held, width), 0, 0)
            total = total.astype(jnp.bfloat16)
            for q in range(4):
                part_ref[a, q, j] = total[q * quarter : (q + 1) * quarter]
            far[a, j] = remote(
                part_ref.at[a, diagonal, j], near.at[a, 0, j], add_send.at[a, 0, j],
                add_recv.at[a, 0, j], place(replica=core),
            )
            close[a, j] = remote(
                part_ref.at[a, core, j], near.at[a, 1, j], add_send.at[a, 1, j],
                add_recv.at[a, 1, j], place(replica=core),
            )

    def add_near(a):
        for j in order:
            far[a, j].wait_recv()
            total = wide(part_ref[a, across, j]) + wide(near[a, 0, j])
            crossing[a, j] = total.astype(jnp.bfloat16)
            cross[a, j] = remote(
                crossing.at[a, j], crossed.at[a, j], add_send.at[a, 2, j], add_recv.at[a, 2, j],
                place(replica=across),
            )

    def add_crossed(a):
        for j in order:
            close[a, j].wait_recv()
            cross[a, j].wait_recv()
            total = wide(part_ref[a, r, j]) + wide(near[a, 1, j]) + wide(crossed[a, j])
            summed[a, j] = total.astype(jnp.bfloat16)
            if j > 0:
                along[a, j] = remote(
                    summed.at[a, j], arrived.at[a, j], add_send.at[a, 3, j], add_recv.at[a, 3, j],
                    place(expert=where[j]),
                )

    def add_along(a):
        for j in (1, 2, 3):
            along[a, j].wait_recv()
        total = wide(summed[a, 0]) + wide(arrived[a, 1])
        total = total + wide(arrived[a, 2]) + wide(arrived[a, 3])
        final[a, r] = total.astype(jnp.bfloat16)
        own = final.at[a, r]
        end[a, 0] = remote(
            own, own, add_send.at[a, 4, 0], add_recv.at[a, 4, 0], place(replica=across)
        )
        end[a, 1] = remote(
            own, own, add_send.at[a, 4, 1], add_recv.at[a, 4, 1], place(replica=core)
        )

    def hand_on(a):
        end[a, 0].wait_recv()
        got = final.at[a, across]
        end[a, 2] = remote(
            got, got, add_send.at[a, 4, 2], add_recv.at[a, 4, 2], place(replica=core)
        )

    def finish(a, target):
        end[a, 1].wait_recv()
        end[a, 2].wait_recv()
        for q in range(4):
            target[q * quarter : (q + 1) * quarter, :] = final[a, q]

    for j in (1, 2, 3):
        metas[j].wait_recv()
    choose()
    pass_on(0)
    pass_last(0)
    pass_on(1)
    received(0)
    take(0, x_rows)
    some = slots // 4
    lax.fori_loop(0, some, forward, 0)
    pass_last(1)
    lax.fori_loop(some, slots, forward, 0)
    gather_back(0)
    received(1)
    take(1, g_rows)
    add_near(0)
    lax.fori_loop(0, slots // 2, backward, 0)
    add_crossed(0)
    lax.fori_loop(slots // 2, slots, backward, 0)
    gather_back(1)
    back, forth = {}, {}
    names = slot_names()
    for b in range(4):
        pick = wide(pick_ref[b]).reshape(slots, MOST, block)
        inner_of = jnp.sum(pick * inner_ref[:, b], axis=1)
        for k in range(top):
            same = meta_ref[b, k : k + 1, :] == names
            prob_ref[b, k : k + 1, :] = jnp.sum(
                jnp.where(same, inner_of, 0.0), axis=0, keepdims=True
            )
        prob_ref[b, top:8, :] = jnp.zeros((8 - top, block), jnp.float32)
    for j in (1, 2, 3):
        back[j] = remote(
            prob_ref.at[where[j]], prob_in.at[j], prob_send.at[0, j], prob_recv.at[0, j],
            place(expert=where[j]),
        )
    add_near(1)
    add_along(0)
    hand_on(0)
    add_crossed(1)
    for j in (1, 2, 3):
        back[j].wait_recv()
    prob_all[r] = prob_ref[e] + prob_in[1] + prob_in[2] + prob_in[3]
    for i in (1, 2, 3):
        forth[i] = remote(
            prob_all.at[r], prob_all.at[r], prob_send.at[1, i], prob_recv.at[1, i],
            place(replica=lax.rem(r + i, 4)),
        )
    finish(0, layer_ref)
    add_along(1)
    for i in (1, 2, 3):
        forth[i].wait()
    prob_out[...] = prob_all[0] + prob_all[1] + prob_all[2] + prob_all[3]
    hand_on(1)
    finish(1, token_ref)
    for j in (1, 2, 3):
        metas[j].wait_send()
        back[j].wait_send()
    for a in (0, 1):
        for j in (1, 2, 3):
            first[a, j].wait_send()
            passed[a, j].wait_send()
            spread[a, j].wait_send()
            last[a, j].wait_send()
            along[a, j].wait_send()
        for j in order:
            far[a, j].wait_send()
            close[a, j].wait_send()
            cross[a, j].wait_send()
        for i in range(3):
            end[a, i].wait_send()


def route_pass(tokens, out_grad, meta, gate_weight, up_weight, down_weight):
    slots, units, width = gate_weight.shape
    block = tokens.shape[0]
    rows = 4 * MOST
    half = jnp.bfloat16
    piece = (4, block // 4, width)
    whole = pl.BlockSpec(memory_space=pltpu.VMEM)
    left = pl.BlockSpec(memory_space=pl.ANY)
    return pl.pallas_call(
        route_kernel,
        out_shape=(
            jax.ShapeDtypeStruct((block, width), half),
            jax.ShapeDtypeStruct((block, width), half),
            jax.ShapeDtypeStruct((8, block), jnp.float32),
            jax.ShapeDtypeStruct((slots, 4, MOST, width), half),
            jax.ShapeDtypeStruct((slots, 4, MOST, width), half),
            jax.ShapeDtypeStruct((slots, rows, units), half),
            jax.ShapeDtypeStruct((slots, rows, units), half),
            jax.ShapeDtypeStruct((slots, rows, units), half),
        ),
        in_specs=[whole, whole, whole, left, left, left],
        out_specs=[whole] * 8,
        scratch_shapes=[
            pltpu.VMEM((2, 4, block, width), half),
            pltpu.VMEM((4,) + meta.shape, jnp.float32),
            pltpu.VMEM((slots, units, width), half),
            pltpu.VMEM((slots, units, width), half),
            pltpu.VMEM((slots, units, width), half),
            pltpu.VMEM((slots, rows, units), jnp.float32),
            pltpu.VMEM((slots, rows, units), jnp.float32),
            pltpu.VMEM((4, slots, MOST, width), half),
            pltpu.VMEM((4, slots * MOST, block), half),
            pltpu.VMEM((slots, 4, MOST, 1), jnp.float32),
            pltpu.VMEM((slots, 4, MOST, 1), jnp.float32),
            pltpu.VMEM((2, 4) + piece, half),
            pltpu.VMEM((2, 2) + piece, half),
            pltpu.VMEM((2,) + piece, half),
            pltpu.VMEM((2,) + piece, half),
            pltpu.VMEM((2,) + piece, half),
            pltpu.VMEM((2,) + piece, half),
            pltpu.VMEM((2,) + piece, half),
            pltpu.VMEM((4, 8, block), jnp.float32),
            pltpu.VMEM((4, 8, block), jnp.float32),
            pltpu.VMEM((4, 8, block), jnp.float32),
            pltpu.SemaphoreType.DMA((3, slots)),
            pltpu.SemaphoreType.DMA((2, 5, 4)),
            pltpu.SemaphoreType.DMA((2, 5, 4)),
            pltpu.SemaphoreType.DMA((2, 5, 4)),
            pltpu.SemaphoreType.DMA((2, 5, 4)),
            pltpu.SemaphoreType.DMA((2, 4)),
            pltpu.SemaphoreType.DMA((2, 4)),
        ],
        compiler_params=pltpu.CompilerParams(
            collective_id=0, has_side_effects=True, vmem_limit_bytes=61 * 2**20
        ),
    )(tokens, out_grad, meta, gate_weight, up_weight, down_weight)


def grad_kernel(
    x_ref, g_ref, scaled_ref, gate_back_ref, up_back_ref, gate_out, up_out, down_out
):
    x, g = x_ref[0], g_ref[0]
    gate_out[0] = dot(gate_back_ref[0], x, 0, 0).astype(jnp.bfloat16)
    up_out[0] = dot(up_back_ref[0], x, 0, 0).astype(jnp.bfloat16)
    down_out[0] = dot(scaled_ref[0], g, 0, 0).astype(jnp.bfloat16)


def grad_pass(x_rows, g_rows, scaled, gate_back, up_back):
    slots, rows, units = scaled.shape
    width = x_rows.shape[-1]
    x_rows = x_rows.reshape(slots, rows, width)
    g_rows = g_rows.reshape(slots, rows, width)
    long = pl.BlockSpec((1, rows, width), lambda s: (s, 0, 0))
    short = pl.BlockSpec((1, rows, units), lambda s: (s, 0, 0))
    wide = pl.BlockSpec((1, units, width), lambda s: (s, 0, 0))
    return pl.pallas_call(
        grad_kernel,
        grid=(slots,),
        out_shape=(jax.ShapeDtypeStruct((slots, units, width), jnp.bfloat16),) * 3,
        in_specs=[long, long, short, short, short],
        out_specs=[wide] * 3,
        compiler_params=pltpu.CompilerParams(vmem_limit_bytes=32 * 2**20),
    )(x_rows, g_rows, scaled, gate_back, up_back)


def gathered_shards(
    tokens, out_grad, route_probs, routes, placement, gate_weight, up_weight, down_weight
):
    block, top_k = routes.shape
    expert_ids = jnp.arange(placement.shape[0], dtype=jnp.int32)
    matches = routes.T[:, :, None] == expert_ids
    slot_ids = jnp.sum(jnp.where(matches, placement, 0), axis=2, dtype=jnp.int32)
    fill = ((0, 8 - top_k), (0, 0))
    meta = jnp.concatenate(
        [
            jnp.pad(slot_ids.astype(jnp.float32), fill, constant_values=-1.0),
            jnp.pad(route_probs.T, fill),
        ],
        axis=0,
    )
    layer_out, token_grad, prob_sum, *kept = route_pass(
        tokens,
        out_grad,
        meta,
        jnp.swapaxes(gate_weight, 1, 2),
        jnp.swapaxes(up_weight, 1, 2),
        down_weight,
    )
    gate_grad, up_grad, down_grad = grad_pass(*kept)
    gate_grad, up_grad = jnp.swapaxes(gate_grad, 1, 2), jnp.swapaxes(up_grad, 1, 2)
    return (layer_out, token_grad, prob_sum[:top_k].T, gate_grad, up_grad, down_grad)


def solution(mesh):
    in_specs = (
        P(("groups", "expert"), None),
        P(("groups", "expert"), None),
        P(("groups", "expert"), None),
        P(("groups", "expert"), None),
        P(),
        P("expert", None, "replica"),
        P("expert", None, "replica"),
        P("expert", "replica", None),
    )
    out_specs = (
        P(("groups", "expert"), None),
        P(("groups", "expert"), None),
        P(("groups", "expert"), None),
        P(("groups", "expert"), None, "replica"),
        P(("groups", "expert"), None, "replica"),
        P(("groups", "expert"), "replica", None),
    )
    small = mesh.shape["expert"] == 4 and mesh.shape["replica"] == 4
    body = gathered_shards if small else shards
    return jax.shard_map(body, mesh=mesh, in_specs=in_specs, out_specs=out_specs, check_vma=False)
```

```python
import jax
import jax.numpy as jnp
from jax import lax
from jax.experimental import pallas as pl
from jax.experimental.pallas import tpu as pltpu
from jax.sharding import PartitionSpec as P

MOST = 16
MESH = pl.DeviceIdType.MESH


def expert_rows(input_rows, back_rows, gate_weight, up_weight, down_weight):
    gate_pre = jnp.einsum(
        "slcd,ldh->slch", input_rows, gate_weight, preferred_element_type=jnp.float32
    )
    up_pre = jnp.einsum("slcd,ldh->slch", input_rows, up_weight, preferred_element_type=jnp.float32)
    sigma_gate = jax.nn.sigmoid(gate_pre)
    swish_gate = gate_pre * sigma_gate
    hidden = (swish_gate * up_pre).astype(jnp.bfloat16)
    outputs = jnp.einsum("slch,lhd->slcd", hidden, down_weight, preferred_element_type=jnp.float32)
    hidden_grad = jnp.einsum(
        "slcd,lhd->slch", back_rows, down_weight, preferred_element_type=jnp.float32
    )
    gate_back = (hidden_grad * up_pre * sigma_gate * (1.0 + gate_pre * (1.0 - sigma_gate))).astype(
        jnp.bfloat16
    )
    up_back = (hidden_grad * swish_gate).astype(jnp.bfloat16)
    input_grad = jnp.einsum(
        "slch,ldh->slcd", gate_back, gate_weight, preferred_element_type=jnp.float32
    )
    input_grad = input_grad + jnp.einsum(
        "slch,ldh->slcd", up_back, up_weight, preferred_element_type=jnp.float32
    )
    return (outputs, input_grad, hidden, gate_back, up_back)


def shards(tokens, out_grad, route_probs, routes, placement, gate_weight, up_weight, down_weight):
    local_experts = gate_weight.shape[0]
    index_count = lax.axis_size("expert")
    experts_all = placement.shape[0]
    tok_rows, top_k = routes.shape
    model_width = tokens.shape[1]
    capacity = MOST
    expert_ids = jnp.arange(experts_all, dtype=jnp.int32)
    match_table = routes.reshape(-1)[:, None] == expert_ids[None, :]
    slot_ids = jnp.sum(jnp.where(match_table, placement[None, :], 0), axis=1, dtype=jnp.int32)
    slot_match = (slot_ids[:, None] == expert_ids[None, :]).astype(jnp.int32)
    rank_ids = jnp.sum(
        (jnp.cumsum(slot_match, axis=0, dtype=jnp.int32) - 1) * slot_match, axis=1, dtype=jnp.int32
    )
    position = slot_ids * capacity + rank_ids
    route_count = tok_rows * top_k
    buffer_rows = experts_all * capacity
    route_of = (
        jnp.full((buffer_rows,), route_count, jnp.int32)
        .at[position]
        .set(jnp.arange(route_count, dtype=jnp.int32))
    )
    filled = route_of < route_count
    safe_route = jnp.where(filled, route_of, 0)
    token_of = safe_route // top_k
    probs_flat = route_probs.reshape(-1)
    input_send = jnp.where(filled[:, None], tokens[token_of], jnp.zeros((), jnp.bfloat16))
    scaled = probs_flat[safe_route][:, None] * out_grad[token_of].astype(jnp.float32)
    back_send = jnp.where(filled[:, None], scaled, 0.0).astype(jnp.bfloat16)
    buffer_shape = (index_count, local_experts, capacity, model_width)
    input_send = input_send.reshape(buffer_shape)
    back_send = back_send.reshape(buffer_shape)
    input_piece = lax.all_to_all(input_send, "expert", split_axis=0, concat_axis=0, tiled=True)
    back_piece = lax.all_to_all(back_send, "expert", split_axis=0, concat_axis=0, tiled=True)
    results = expert_rows(input_piece, back_piece, gate_weight, up_weight, down_weight)
    input_rows, back_rows, outputs, input_grad, hidden, gate_back, up_back = (
        input_piece,
        back_piece,
    ) + results
    gate_grad = jnp.einsum(
        "slcd,slch->ldh", input_rows, gate_back, preferred_element_type=jnp.float32
    ).astype(jnp.bfloat16)
    up_grad = jnp.einsum(
        "slcd,slch->ldh", input_rows, up_back, preferred_element_type=jnp.float32
    ).astype(jnp.bfloat16)
    down_grad = jnp.einsum(
        "slch,slcd->lhd", hidden, back_rows, preferred_element_type=jnp.float32
    ).astype(jnp.bfloat16)
    out_back, grad_back = (
        lax.all_to_all(
            outputs.astype(jnp.bfloat16), "expert", split_axis=0, concat_axis=0, tiled=True
        ),
        lax.all_to_all(
            input_grad.astype(jnp.bfloat16), "expert", split_axis=0, concat_axis=0, tiled=True
        ),
    )
    kept_mask = rank_ids >= 0
    out_rows = out_back.reshape(-1, model_width)[position].astype(jnp.float32)
    grad_rows = grad_back.reshape(-1, model_width)[position].astype(jnp.float32)
    kept_rows = kept_mask.reshape(tok_rows, top_k)
    route_weight = jnp.where(kept_mask, probs_flat, 0.0).reshape(tok_rows, top_k)
    out_rows = out_rows.reshape(tok_rows, top_k, model_width)
    grad_rows = grad_rows.reshape(tok_rows, top_k, model_width)
    layer_part = jnp.sum(route_weight[:, :, None] * out_rows, axis=1)
    token_part = jnp.sum(jnp.where(kept_rows[:, :, None], grad_rows, 0.0), axis=1)
    prob_part = jnp.where(
        kept_rows, jnp.sum(out_grad.astype(jnp.float32)[:, None, :] * out_rows, axis=2), 0.0
    )
    layer_sum, token_sum, prob_sum = (
        lax.psum(layer_part.astype(jnp.bfloat16), "replica").astype(jnp.float32),
        lax.psum(token_part.astype(jnp.bfloat16), "replica").astype(jnp.float32),
        lax.psum(prob_part.astype(jnp.bfloat16), "replica").astype(jnp.float32),
    )
    return (
        layer_sum.astype(jnp.bfloat16),
        token_sum.astype(jnp.bfloat16),
        prob_sum,
        gate_grad,
        up_grad,
        down_grad,
    )


def place(expert=None, replica=None):
    own = [lax.axis_index("groups"), lax.axis_index("expert"), lax.axis_index("replica")]
    if expert is not None:
        own[1] = expert
    if replica is not None:
        own[2] = replica
    return tuple(own)


def greet(devices):
    barrier = pltpu.get_barrier_semaphore()
    for device in devices:
        pl.semaphore_signal(barrier, inc=1, device_id=device, device_id_type=MESH)
    pl.semaphore_wait(barrier, len(devices))


def positions():
    e, r = lax.axis_index("expert"), lax.axis_index("replica")
    core = r + 1 - 2 * lax.rem(r, 2)
    across = lax.rem(r + 2, 4)
    diagonal = lax.rem(core + 2, 4)
    return e, r, core, across, diagonal


def remote(src, dst, send, recv, device):
    copy = pltpu.make_async_remote_copy(
        src_ref=src, dst_ref=dst, send_sem=send, recv_sem=recv, device_id=device, device_id_type=MESH
    )
    copy.start()
    return copy


def dot(left, right, left_dim, right_dim):
    return lax.dot_general(
        left, right, (((left_dim,), (right_dim,)), ((), ())), preferred_element_type=jnp.float32
    )

def route_kernel(
    x_ref, g_ref, m_ref, gate_hbm, up_hbm, down_hbm,
    layer_ref, token_ref, prob_out, x_hbm, g_hbm, scaled_hbm, gate_back_hbm, up_back_hbm,
    x_rows, g_rows, scaled_ref, gate_back_ref, up_back_ref,
    rows_ref, meta_ref, gate_ref, up_ref, down_ref, gate_pre_ref, up_pre_ref, back_rows,
    pick_ref, weight_ref, inner_ref, part_ref, near, crossing, crossed, summed, arrived, final,
    prob_ref, prob_in, prob_all, load, saved, send, recv, add_send, add_recv, prob_send, prob_recv,
):
    e, r, core, across, diagonal = positions()
    slots, units, width = gate_ref.shape
    block = x_ref.shape[0]
    quarter = block // 4
    top = 6
    held = slots * MOST
    rows = 4 * MOST
    mine = pl.ds(pl.multiple_of(r * quarter, quarter), quarter)
    other = pl.ds(pl.multiple_of(across * quarter, quarter), quarter)
    weights = ((gate_hbm, gate_ref), (up_hbm, up_ref), (down_hbm, down_ref))

    kept = []
    results = (
        (x_rows, x_hbm), (g_rows, g_hbm), (scaled_ref, scaled_hbm),
        (gate_back_ref, gate_back_hbm), (up_back_ref, up_back_hbm),
    )

    def store(i):
        copy = pltpu.make_async_copy(results[i][0], results[i][1], saved.at[i])
        copy.start()
        return copy

    def fetch(s, start):
        for i, (source, target) in enumerate(weights):
            copy = pltpu.make_async_copy(source.at[s], target.at[s], load.at[i, s])
            if start:
                copy.start()
            else:
                copy.wait()

    def start_fetch(s, carry):
        fetch(s, True)
        return carry

    lax.fori_loop(0, slots, start_fetch, 0)
    rows_ref[0, e] = x_ref[...]
    rows_ref[1, e] = g_ref[...]
    meta_ref[e] = m_ref[...]
    greet(
        [place(expert=lax.rem(e + j, 4)) for j in (1, 2, 3)]
        + [place(replica=lax.rem(r + i, 4)) for i in (1, 2, 3)]
    )
    metas, first, passed, spread, last = {}, {}, {}, {}, {}
    for j in (2, 1, 3):
        peer = place(expert=lax.rem(e + j, 4))
        metas[j] = remote(meta_ref.at[e], meta_ref.at[e], send.at[0, 0, j], recv.at[0, 0, j], peer)
    for a in (0, 1):
        for j in (2, 1, 3):
            peer = place(expert=lax.rem(e + j, 4))
            own = rows_ref.at[a, e, mine]
            first[a, j] = remote(own, own, send.at[a, 1, j], recv.at[a, 1, j], peer)

    def pass_on(a):
        for j in (1, 3, 2):
            first[a, j].wait_recv()
            part = rows_ref.at[a, lax.rem(e + 4 - j, 4), mine]
            passed[a, j] = remote(
                part, part, send.at[a, 2, j], recv.at[a, 2, j], place(replica=across)
            )
            spread[a, j] = remote(
                part, part, send.at[a, 3, j], recv.at[a, 3, j], place(replica=core)
            )

    def pass_last(a):
        for j in (1, 3, 2):
            passed[a, j].wait_recv()
            part = rows_ref.at[a, lax.rem(e + 4 - j, 4), other]
            last[a, j] = remote(part, part, send.at[a, 4, j], recv.at[a, 4, j], place(replica=core))

    def received(a):
        for j in (1, 3, 2):
            spread[a, j].wait_recv()
            last[a, j].wait_recv()

    def slot_names():
        names = lax.broadcasted_iota(jnp.int32, (slots, block), 0) + e * slots
        return names.astype(jnp.float32)

    def wide(value):
        return value.astype(jnp.float32)

    def choose():
        names = slot_names()
        before = lax.broadcasted_iota(jnp.int32, (block, block), 0)
        after = lax.broadcasted_iota(jnp.int32, (block, block), 1)
        earlier = (before < after).astype(jnp.float32).astype(jnp.bfloat16)
        ranks = lax.broadcasted_iota(jnp.int32, (slots, MOST, block), 1).astype(jnp.float32)
        for b in range(4):
            named = jnp.zeros((slots, block), jnp.float32)
            probs = jnp.zeros((slots, block), jnp.float32)
            for k in range(top):
                same = meta_ref[b, k : k + 1, :] == names
                named = named + jnp.where(same, 1.0, 0.0)
                probs = probs + jnp.where(same, meta_ref[b, 8 + k : 9 + k, :], 0.0)
            rank = dot(named.astype(jnp.bfloat16), earlier, 1, 0)
            rank = jnp.where(named > 0.0, rank, -1.0)
            pick = jnp.where(rank[:, None, :] == ranks, 1.0, 0.0)
            weight_ref[:, b] = jnp.sum(pick * probs[:, None, :], axis=2, keepdims=True)
            pick_ref[b] = pick.reshape(held, block).astype(jnp.bfloat16)

    def take(a, target):
        for b in range(4):
            target[:, b] = (
                dot(pick_ref[b], rows_ref[a, b], 1, 0)
                .astype(jnp.bfloat16)
                .reshape(slots, MOST, width)
            )

    def keep(s, value):
        value = value.astype(jnp.bfloat16).reshape(4, MOST, width)
        for b in range(4):
            back_rows[b, s] = value[b]

    def forward(pair, carry):
        both = (2 * pair, 2 * pair + 1)
        for s in both:
            fetch(s, False)
        x = [x_rows[s].reshape(rows, width) for s in both]
        gate_pre = [dot(x[i], gate_ref[s], 1, 1) for i, s in enumerate(both)]
        up_pre = [dot(x[i], up_ref[s], 1, 1) for i, s in enumerate(both)]
        scaled = []
        for i, s in enumerate(both):
            swish = gate_pre[i] * jax.nn.sigmoid(gate_pre[i])
            hidden = wide((swish * up_pre[i]).astype(jnp.bfloat16))
            scaled.append((hidden * weight_ref[s].reshape(rows, 1)).astype(jnp.bfloat16))
        output = [dot(scaled[i], down_ref[s], 1, 0) for i, s in enumerate(both)]
        for i, s in enumerate(both):
            gate_pre_ref[s] = gate_pre[i]
            up_pre_ref[s] = up_pre[i]
            scaled_ref[s] = scaled[i]
            keep(s, output[i])
        return carry

    def backward(pair, carry):
        both = (2 * pair, 2 * pair + 1)
        plain_grad = [dot(g_rows[s].reshape(rows, width), down_ref[s], 1, 1) for s in both]
        gate_back, up_back, inner = [], [], []
        for i, s in enumerate(both):
            gate_pre, up_pre = gate_pre_ref[s], up_pre_ref[s]
            sigma = jax.nn.sigmoid(gate_pre)
            swish = gate_pre * sigma
            hidden = wide((swish * up_pre).astype(jnp.bfloat16))
            inner.append(jnp.sum(hidden * plain_grad[i], axis=1, keepdims=True))
            hidden_grad = plain_grad[i] * weight_ref[s].reshape(rows, 1)
            slope = sigma * (1.0 + gate_pre * (1.0 - sigma))
            gate_back.append((hidden_grad * up_pre * slope).astype(jnp.bfloat16))
            up_back.append((hidden_grad * swish).astype(jnp.bfloat16))
        input_grad = [
            dot(gate_back[i], gate_ref[s], 1, 0) + dot(up_back[i], up_ref[s], 1, 0)
            for i, s in enumerate(both)
        ]
        for i, s in enumerate(both):
            inner_ref[s] = inner[i].reshape(4, MOST, 1)
            gate_back_ref[s] = gate_back[i]
            up_back_ref[s] = up_back[i]
            keep(s, input_grad[i])
        return carry

    order = (2, 1, 3, 0)
    where = [lax.rem(e + j, 4) for j in range(4)]
    far, close, cross, along, end = {}, {}, {}, {}, {}

    def gather_back(a):
        for j in order:
            total = dot(pick_ref[where[j]], back_rows[where[j]].reshape(held, width), 0, 0)
            total = total.astype(jnp.bfloat16)
            for q in range(4):
                part_ref[a, q, j] = total[q * quarter : (q + 1) * quarter]
            far[a, j] = remote(
                part_ref.at[a, diagonal, j], near.at[a, 0, j], add_send.at[a, 0, j],
                add_recv.at[a, 0, j], place(replica=core),
            )
            close[a, j] = remote(
                part_ref.at[a, core, j], near.at[a, 1, j], add_send.at[a, 1, j],
                add_recv.at[a, 1, j], place(replica=core),
            )

    def add_near(a):
        for j in order:
            far[a, j].wait_recv()
            total = wide(part_ref[a, across, j]) + wide(near[a, 0, j])
            crossing[a, j] = total.astype(jnp.bfloat16)
            cross[a, j] = remote(
                crossing.at[a, j], crossed.at[a, j], add_send.at[a, 2, j], add_recv.at[a, 2, j],
                place(replica=across),
            )

    def add_crossed(a):
        for j in order:
            close[a, j].wait_recv()
            cross[a, j].wait_recv()
            total = wide(part_ref[a, r, j]) + wide(near[a, 1, j]) + wide(crossed[a, j])
            summed[a, j] = total.astype(jnp.bfloat16)
            if j > 0:
                along[a, j] = remote(
                    summed.at[a, j], arrived.at[a, j], add_send.at[a, 3, j], add_recv.at[a, 3, j],
                    place(expert=where[j]),
                )

    def add_along(a):
        for j in (1, 2, 3):
            along[a, j].wait_recv()
        total = wide(summed[a, 0]) + wide(arrived[a, 1])
        total = total + wide(arrived[a, 2]) + wide(arrived[a, 3])
        final[a, r] = total.astype(jnp.bfloat16)
        own = final.at[a, r]
        end[a, 0] = remote(
            own, own, add_send.at[a, 4, 0], add_recv.at[a, 4, 0], place(replica=across)
        )
        end[a, 1] = remote(
            own, own, add_send.at[a, 4, 1], add_recv.at[a, 4, 1], place(replica=core)
        )

    def hand_on(a):
        end[a, 0].wait_recv()
        got = final.at[a, across]
        end[a, 2] = remote(
            got, got, add_send.at[a, 4, 2], add_recv.at[a, 4, 2], place(replica=core)
        )

    def finish(a, target):
        end[a, 1].wait_recv()
        end[a, 2].wait_recv()
        for q in range(4):
            target[q * quarter : (q + 1) * quarter, :] = final[a, q]

    for j in (1, 2, 3):
        metas[j].wait_recv()
    choose()
    pass_on(0)
    pass_last(0)
    pass_on(1)
    received(0)
    take(0, x_rows)
    kept.append(store(0))
    pairs = slots // 2
    some = pairs // 4
    lax.fori_loop(0, some, forward, 0)
    pass_last(1)
    lax.fori_loop(some, pairs, forward, 0)
    kept.append(store(2))
    gather_back(0)
    received(1)
    take(1, g_rows)
    kept.append(store(1))
    add_near(0)
    lax.fori_loop(0, pairs // 2, backward, 0)
    add_crossed(0)
    lax.fori_loop(pairs // 2, pairs, backward, 0)
    kept.append(store(3))
    kept.append(store(4))
    gather_back(1)
    back, forth = {}, {}
    names = slot_names()
    for b in range(4):
        pick = wide(pick_ref[b]).reshape(slots, MOST, block)
        inner_of = jnp.sum(pick * inner_ref[:, b], axis=1)
        for k in range(top):
            same = meta_ref[b, k : k + 1, :] == names
            prob_ref[b, k : k + 1, :] = jnp.sum(
                jnp.where(same, inner_of, 0.0), axis=0, keepdims=True
            )
        prob_ref[b, top:8, :] = jnp.zeros((8 - top, block), jnp.float32)
    for j in (1, 2, 3):
        back[j] = remote(
            prob_ref.at[where[j]], prob_in.at[j], prob_send.at[0, j], prob_recv.at[0, j],
            place(expert=where[j]),
        )
    add_near(1)
    add_along(0)
    hand_on(0)
    add_crossed(1)
    for j in (1, 2, 3):
        back[j].wait_recv()
    prob_all[r] = prob_ref[e] + prob_in[1] + prob_in[2] + prob_in[3]
    for i in (1, 2, 3):
        forth[i] = remote(
            prob_all.at[r], prob_all.at[r], prob_send.at[1, i], prob_recv.at[1, i],
            place(replica=lax.rem(r + i, 4)),
        )
    finish(0, layer_ref)
    add_along(1)
    for i in (1, 2, 3):
        forth[i].wait()
    prob_out[...] = prob_all[0] + prob_all[1] + prob_all[2] + prob_all[3]
    hand_on(1)
    finish(1, token_ref)
    for copy in kept:
        copy.wait()
    for j in (1, 2, 3):
        metas[j].wait_send()
        back[j].wait_send()
    for a in (0, 1):
        for j in (1, 2, 3):
            first[a, j].wait_send()
            passed[a, j].wait_send()
            spread[a, j].wait_send()
            last[a, j].wait_send()
            along[a, j].wait_send()
        for j in order:
            far[a, j].wait_send()
            close[a, j].wait_send()
            cross[a, j].wait_send()
        for i in range(3):
            end[a, i].wait_send()


def route_pass(tokens, out_grad, meta, gate_weight, up_weight, down_weight):
    slots, units, width = gate_weight.shape
    block = tokens.shape[0]
    rows = 4 * MOST
    half = jnp.bfloat16
    piece = (4, block // 4, width)
    whole = pl.BlockSpec(memory_space=pltpu.VMEM)
    left = pl.BlockSpec(memory_space=pl.ANY)
    return pl.pallas_call(
        route_kernel,
        out_shape=(
            jax.ShapeDtypeStruct((block, width), half),
            jax.ShapeDtypeStruct((block, width), half),
            jax.ShapeDtypeStruct((8, block), jnp.float32),
            jax.ShapeDtypeStruct((slots, 4, MOST, width), half),
            jax.ShapeDtypeStruct((slots, 4, MOST, width), half),
            jax.ShapeDtypeStruct((slots, rows, units), half),
            jax.ShapeDtypeStruct((slots, rows, units), half),
            jax.ShapeDtypeStruct((slots, rows, units), half),
        ),
        in_specs=[whole, whole, whole, left, left, left],
        out_specs=[whole] * 3 + [left] * 5,
        scratch_shapes=[
            pltpu.VMEM((slots, 4, MOST, width), half),
            pltpu.VMEM((slots, 4, MOST, width), half),
            pltpu.VMEM((slots, rows, units), half),
            pltpu.VMEM((slots, rows, units), half),
            pltpu.VMEM((slots, rows, units), half),
            pltpu.VMEM((2, 4, block, width), half),
            pltpu.VMEM((4,) + meta.shape, jnp.float32),
            pltpu.VMEM((slots, units, width), half),
            pltpu.VMEM((slots, units, width), half),
            pltpu.VMEM((slots, units, width), half),
            pltpu.VMEM((slots, rows, units), jnp.float32),
            pltpu.VMEM((slots, rows, units), jnp.float32),
            pltpu.VMEM((4, slots, MOST, width), half),
            pltpu.VMEM((4, slots * MOST, block), half),
            pltpu.VMEM((slots, 4, MOST, 1), jnp.float32),
            pltpu.VMEM((slots, 4, MOST, 1), jnp.float32),
            pltpu.VMEM((2, 4) + piece, half),
            pltpu.VMEM((2, 2) + piece, half),
            pltpu.VMEM((2,) + piece, half),
            pltpu.VMEM((2,) + piece, half),
            pltpu.VMEM((2,) + piece, half),
            pltpu.VMEM((2,) + piece, half),
            pltpu.VMEM((2,) + piece, half),
            pltpu.VMEM((4, 8, block), jnp.float32),
            pltpu.VMEM((4, 8, block), jnp.float32),
            pltpu.VMEM((4, 8, block), jnp.float32),
            pltpu.SemaphoreType.DMA((3, slots)),
            pltpu.SemaphoreType.DMA((5,)),
            pltpu.SemaphoreType.DMA((2, 5, 4)),
            pltpu.SemaphoreType.DMA((2, 5, 4)),
            pltpu.SemaphoreType.DMA((2, 5, 4)),
            pltpu.SemaphoreType.DMA((2, 5, 4)),
            pltpu.SemaphoreType.DMA((2, 4)),
            pltpu.SemaphoreType.DMA((2, 4)),
        ],
        compiler_params=pltpu.CompilerParams(
            collective_id=0, has_side_effects=True, vmem_limit_bytes=61 * 2**20
        ),
    )(tokens, out_grad, meta, gate_weight, up_weight, down_weight)


def grad_kernel(
    x_ref, g_ref, scaled_ref, gate_back_ref, up_back_ref, gate_out, up_out, down_out
):
    x, g = x_ref[0], g_ref[0]
    gate_out[0] = dot(gate_back_ref[0], x, 0, 0).astype(jnp.bfloat16)
    up_out[0] = dot(up_back_ref[0], x, 0, 0).astype(jnp.bfloat16)
    down_out[0] = dot(scaled_ref[0], g, 0, 0).astype(jnp.bfloat16)


def grad_pass(x_rows, g_rows, scaled, gate_back, up_back):
    slots, rows, units = scaled.shape
    width = x_rows.shape[-1]
    x_rows = x_rows.reshape(slots, rows, width)
    g_rows = g_rows.reshape(slots, rows, width)
    long = pl.BlockSpec((1, rows, width), lambda s: (s, 0, 0))
    short = pl.BlockSpec((1, rows, units), lambda s: (s, 0, 0))
    wide = pl.BlockSpec((1, units, width), lambda s: (s, 0, 0))
    return pl.pallas_call(
        grad_kernel,
        grid=(slots,),
        out_shape=(jax.ShapeDtypeStruct((slots, units, width), jnp.bfloat16),) * 3,
        in_specs=[long, long, short, short, short],
        out_specs=[wide] * 3,
        compiler_params=pltpu.CompilerParams(vmem_limit_bytes=60 * 2**20),
    )(x_rows, g_rows, scaled, gate_back, up_back)


def gathered_shards(
    tokens, out_grad, route_probs, routes, placement, gate_weight, up_weight, down_weight
):
    block, top_k = routes.shape
    expert_ids = jnp.arange(placement.shape[0], dtype=jnp.int32)
    matches = routes.T[:, :, None] == expert_ids
    slot_ids = jnp.sum(jnp.where(matches, placement, 0), axis=2, dtype=jnp.int32)
    fill = ((0, 8 - top_k), (0, 0))
    meta = jnp.concatenate(
        [
            jnp.pad(slot_ids.astype(jnp.float32), fill, constant_values=-1.0),
            jnp.pad(route_probs.T, fill),
        ],
        axis=0,
    )
    layer_out, token_grad, prob_sum, *kept = route_pass(
        tokens,
        out_grad,
        meta,
        jnp.swapaxes(gate_weight, 1, 2),
        jnp.swapaxes(up_weight, 1, 2),
        down_weight,
    )
    gate_grad, up_grad, down_grad = grad_pass(*kept)
    gate_grad, up_grad = jnp.swapaxes(gate_grad, 1, 2), jnp.swapaxes(up_grad, 1, 2)
    return (layer_out, token_grad, prob_sum[:top_k].T, gate_grad, up_grad, down_grad)


def solution(mesh):
    in_specs = (
        P(("groups", "expert"), None),
        P(("groups", "expert"), None),
        P(("groups", "expert"), None),
        P(("groups", "expert"), None),
        P(),
        P("expert", None, "replica"),
        P("expert", None, "replica"),
        P("expert", "replica", None),
    )
    out_specs = (
        P(("groups", "expert"), None),
        P(("groups", "expert"), None),
        P(("groups", "expert"), None),
        P(("groups", "expert"), None, "replica"),
        P(("groups", "expert"), None, "replica"),
        P(("groups", "expert"), "replica", None),
    )
    small = mesh.shape["expert"] == 4 and mesh.shape["replica"] == 4
    body = gathered_shards if small else shards
    return jax.shard_map(body, mesh=mesh, in_specs=in_specs, out_specs=out_specs, check_vma=False)
```
